512 devices in a mesh: row: 16 (over x, y_hi, core), col: 32 (over y_lo, z).
Axes of the slice: x: 4, y: 8 (y_hi: 2, y_lo: 4; y = y_hi * 4 + y_lo), z: 8, core: 2. Of those that a mesh axis runs over, the one named last changes fastest.
Arguments:
- features: bfloat16 [65536, 512], P(('col', 'row')), may hold values from -6 to 6
- blocks: bfloat16 [16, 32, 48, 128, 128], P('row', 'col'), may hold values from -0.125 to 0.125
- positions: int32 [16, 32, 48], P('row', 'col'), may hold values from 0 to 511, as said below
- counts: int32 [16, 32], P('row', 'col'), may hold values from 8 to 48, as said below
- weight: bfloat16 [512, 512], replicated, may hold values from -0.25 to 0.25
- bias: float32 [512], replicated, may hold values from -3 to 3
- cotangent: bfloat16 [65536, 512], P(('row', 'col')), may hold values from -6 to 6
Outputs:
- activated: bfloat16 [65536, 512], P(('row', 'col'))
- grad_weight: float32 [512, 512], replicated
- grad_bias: float32 [512], replicated
- grad_in: bfloat16 [65536, 512], P(('col', 'row'))
The draws below stay inside these ranges and needn't reach their ends.
Inputs may be any that keep to these rules, and one draw needn't show every extreme that they name: `counts`: every tile uses between 8 and 24 slots, except exactly one tile, which uses all 48. The 48 positions of one tile are distinct; only the first counts[i, j] of them are used.
All inputs are finite; a program needn't handle non-finite values.
Results may differ from the reference program's by a relative error of at most 0.0069.
Values may be sent and summed in bfloat16 or wider, within the bound.
A program may use at most 64 MiB of HBM per device.

```python
import jax
import jax.numpy as jnp
from jax import lax

F = 512
BLOCK = 128
TC = 16
TR = 32
SLOTS = 8
MAXB = 48
NODES = 65536
N_ROW = 16
N_COL = 32


def tile_layout(key):
    key_counts = jax.random.fold_in(key, 11)
    key_heavy = jax.random.fold_in(key, 12)
    key_perm = jax.random.fold_in(key, 13)
    tiles = N_ROW * N_COL
    base_counts = jax.random.randint(key_counts, (tiles,), SLOTS, 3 * SLOTS + 1, dtype=jnp.int32)
    heavy_tile = jax.random.randint(key_heavy, (), 0, tiles, dtype=jnp.int32)
    tile_counts = jnp.where(jnp.arange(tiles, dtype=jnp.int32) == heavy_tile, MAXB, base_counts)
    perm_keys = jax.random.split(key_perm, tiles)
    orders = jax.vmap(lambda one_key: jax.random.permutation(one_key, TR * TC))(perm_keys)
    slot_pos = orders[:, :MAXB].astype(jnp.int32)
    return (tile_counts.astype(jnp.int32).reshape(N_ROW, N_COL), slot_pos.reshape(N_ROW, N_COL, MAXB))


def draw_counts(key, part):
    return tile_layout(key)[0]


def draw_positions(key, part):
    return tile_layout(key)[1]


def level_of(rng, extent, pieces, low, largest):
    loudness, own = 1.0, jax.random.fold_in(rng, 6)
    for dim, parts in pieces:
        steps = jnp.exp(jax.random.uniform(jax.random.fold_in(own, dim), (parts,), jnp.float32, low / len(pieces), largest / len(pieces)))
        loudness = loudness * jnp.repeat(steps, extent[dim] // parts).reshape([-1 if axis == dim else 1 for axis in range(len(extent))])
    return loudness


def normal_values(stream_key, extent, scale, bound, shards=(), kind=jnp.bfloat16):
    values = jax.random.normal(stream_key, extent, jnp.float32) * scale
    if len(shards) > 0:
        values = level_of(stream_key, extent, shards, -0.22, 0.18) * values
    return jnp.clip(values, min=-bound, max=bound).astype(kind)


def setup_inputs(seed: int = 0) -> dict:
    key_of = jax.random.split(jax.random.key(seed), 8)
    return {
        "features": normal_values(key_of[0], (NODES, F), 1.0, 6.0, ((0, 512),)),
        "blocks": normal_values(key_of[1], (N_ROW, N_COL, MAXB, BLOCK, BLOCK), (N_COL * MAXB * BLOCK // (3 * TR)) ** -0.5, 0.125, ((0, 16), (1, 32))),
        "positions": draw_positions(jax.random.fold_in(key_of[7], 71), 0),
        "counts": draw_counts(jax.random.fold_in(key_of[7], 71), 0),
        "weight": normal_values(key_of[4], (F, F), F ** -0.5, 0.25),
        "bias": normal_values(key_of[5], (F,), 0.5, 3.0, (), jnp.float32),
        "cotangent": normal_values(key_of[6], (NODES, F), 1.0, 6.0, ((0, 512),)),
    }


def round_tile(local):
    return lax.optimization_barrier(local.astype(jnp.bfloat16)).astype(jnp.float32)


def forward_tile(i_index, j_index, tile_vals, slot_pos, limit, source_blocks):
    def one_group(group, carried):
        start = (group * SLOTS).astype(jnp.int32)
        block_vals = lax.dynamic_slice_in_dim(tile_vals, start, SLOTS, 0).astype(jnp.float32)
        picked_pos = lax.dynamic_slice_in_dim(slot_pos, start, SLOTS, 0).astype(jnp.int32)
        in_rows = (j_index * TC + picked_pos % TC).astype(jnp.int32)
        alive = ((start + jnp.arange(SLOTS, dtype=jnp.int32)) < limit).astype(jnp.float32)
        picked = source_blocks[in_rows].astype(jnp.float32)
        products = jnp.einsum('sab,sbf->saf', block_vals, picked)
        return carried.at[picked_pos // TC].add(products * alive[:, None, None])

    groups = ((limit + SLOTS - 1) // SLOTS).astype(jnp.int32)
    local = lax.fori_loop(jnp.int32(0), groups, one_group, jnp.zeros((TR, BLOCK, F), jnp.float32))
    return round_tile(local)


def backward_tile(i_index, j_index, tile_vals, slot_pos, limit, source_blocks):
    def one_group(group, carried):
        start = (group * SLOTS).astype(jnp.int32)
        block_vals = lax.dynamic_slice_in_dim(tile_vals, start, SLOTS, 0).astype(jnp.float32)
        picked_pos = lax.dynamic_slice_in_dim(slot_pos, start, SLOTS, 0).astype(jnp.int32)
        out_rows = (i_index * TR + picked_pos // TC).astype(jnp.int32)
        alive = ((start + jnp.arange(SLOTS, dtype=jnp.int32)) < limit).astype(jnp.float32)
        picked = source_blocks[out_rows].astype(jnp.float32)
        products = jnp.einsum('sab,saf->sbf', block_vals, picked)
        return carried.at[picked_pos % TC].add(products * alive[:, None, None])

    groups = ((limit + SLOTS - 1) // SLOTS).astype(jnp.int32)
    local = lax.fori_loop(jnp.int32(0), groups, one_group, jnp.zeros((TC, BLOCK, F), jnp.float32))
    return round_tile(local)


def forward_all(blocks, positions, counts, source):
    source_blocks = source.reshape(NODES // BLOCK, BLOCK, F)

    def one_row(item):
        i_index, row_vals, row_pos, row_counts = item

        def scan_body(totals, inner):
            j_index, tile_vals, slot_pos, limit = inner
            return totals + forward_tile(i_index, j_index, tile_vals, slot_pos, limit, source_blocks), None

        totals, _ = lax.scan(scan_body, jnp.zeros((TR, BLOCK, F), jnp.float32),
                             (jnp.arange(N_COL, dtype=jnp.int32), row_vals, row_pos.astype(jnp.int32),
                              row_counts.astype(jnp.int32)))
        return totals

    result = lax.map(one_row, (jnp.arange(N_ROW, dtype=jnp.int32), blocks, positions, counts))
    return result.reshape(NODES, F)


def backward_all(blocks, positions, counts, source):
    source_blocks = source.reshape(NODES // BLOCK, BLOCK, F)

    def one_column(item):
        j_index, col_vals, col_pos, col_counts = item

        def scan_body(totals, inner):
            i_index, tile_vals, slot_pos, limit = inner
            return totals + backward_tile(i_index, j_index, tile_vals, slot_pos, limit, source_blocks), None

        totals, _ = lax.scan(scan_body, jnp.zeros((TC, BLOCK, F), jnp.float32),
                             (jnp.arange(N_ROW, dtype=jnp.int32), col_vals, col_pos.astype(jnp.int32),
                              col_counts.astype(jnp.int32)))
        return totals

    result = lax.map(one_column, (jnp.arange(N_COL, dtype=jnp.int32), jnp.swapaxes(blocks, 0, 1),
                                  jnp.swapaxes(positions, 0, 1), jnp.swapaxes(counts, 0, 1)))
    return result.reshape(NODES, F)


def reference(features, blocks, positions, counts, weight, bias, cotangent):
    aggregated = forward_all(blocks, positions, counts, features).astype(jnp.bfloat16)
    pre = jnp.dot(aggregated, weight, preferred_element_type=jnp.float32) + bias
    sigma = jax.nn.sigmoid(pre)
    activated = (pre * sigma).astype(jnp.bfloat16)
    grad_pre = (cotangent.astype(jnp.float32) * sigma * (1.0 + pre * (1.0 - sigma))).astype(jnp.bfloat16)
    grad_weight = jnp.dot(aggregated.T, grad_pre, preferred_element_type=jnp.float32)
    grad_bias = jnp.sum(grad_pre.astype(jnp.float32), axis=0)
    grad_mid = jnp.dot(grad_pre, weight.T, preferred_element_type=jnp.float32).astype(jnp.bfloat16)
    grad_in = backward_all(blocks, positions, counts, grad_mid).astype(jnp.bfloat16)
    return activated, grad_weight, grad_bias, grad_in
```

```python
import jax
import jax.numpy as jnp
from jax import lax
from jax.experimental import pallas as pl
from jax.experimental.pallas import tpu as pltpu
from jax.sharding import Mesh
from jax.sharding import PartitionSpec as P

AXES = ("x", "h", "k", "y", "z")
ROW = ("x", "h", "k")
COL = ("y", "z")
ROW_COL = ROW + COL
COL_ROW = COL + ROW
MESH = pl.DeviceIdType.MESH
NX, NH, NK, NY, NZ = 4, 2, 2, 4, 8
TR, TC = NY * NZ, NX * NH * NK
SLOTS = 48
B = 128
HALF = B // 2
F = 512
FC, FP, FL = 0, SLOTS, 2 * SLOTS
BR, BP, BL = FL + TR, FL + TR + SLOTS, FL + TR + 2 * SLOTS
TABLE = BL + TC
BF16, F32 = jnp.bfloat16, jnp.float32


def link_slots(pos, cnt, tab):
    limit = cnt[0]
    for r in range(TR):
        tab[FL + r] = SLOTS
    for c in range(TC):
        tab[BL + c] = SLOTS

    def one(s, carry):
        p = pos[s]
        r, c = lax.div(p, TC), lax.rem(p, TC)
        live = s < limit
        last_r, last_c = tab[FL + r], tab[BL + c]
        tab[FC + s] = c
        tab[BR + s] = r
        tab[FP + s] = last_r
        tab[BP + s] = last_c
        tab[FL + r] = jnp.where(live, s, last_r)
        tab[BL + c] = jnp.where(live, s, last_c)
        return carry

    lax.fori_loop(0, SLOTS, one, 0)


def layer(
    tab, feat, blocks, weight, bias, cot,
    act_out, gw_out, gb_out, gin_out,
    fall, hist, zs1, zr1, zs, zr, ys, yr, sown, agg, mid, ks, kr, xs1, xr1, xs2, xr2, hs, hr,
    g0, gk, gx, gxr, gz, gzr, gy, gyr, gall,
    send, recv,
):
    x, h, k, y, z = (lax.axis_index(a) for a in AXES)

    def at(name, value):
        return {name: value}

    def xo(d):
        return lax.rem(x + d, NX)

    def zo(d):
        return lax.rem(z + d, NZ)

    def yo(d):
        return lax.rem(y + d, NY)

    hy = h * NY + y

    def y8(d):
        place = lax.rem(hy + d, NH * NY)
        return {"h": lax.div(place, NY), "y": lax.rem(place, NY)}

    other = at("k", 1 - k)
    partner = at("h", 1 - h)

    barrier = pltpu.get_barrier_semaphore()
    greeted = [other]
    greeted += [at("x", xo(d)) for d in range(1, NX)]
    greeted += [at("z", zo(d)) for d in range(1, NZ)]
    greeted += [y8(d) for d in range(1, NH * NY)]
    for device in greeted:
        pl.semaphore_signal(barrier, inc=1, device_id=device, device_id_type=MESH)
    pl.semaphore_wait(barrier, len(greeted))

    used = [0]
    pending = []

    def ids(count):
        first = used[0]
        used[0] += count
        return first

    def copy(src, dst, device, n):
        return pltpu.make_async_remote_copy(
            src_ref=src, dst_ref=dst, send_sem=send.at[n], recv_sem=recv.at[n], device_id=device, device_id_type=MESH
        )

    def go(src, dst, device):
        c = copy(src, dst, device, ids(1))
        c.start()
        pending.append(c)
        return c

    def place(xx, hh, kk):
        return xx * (NH * NK) + hh * NK + kk

    fall[place(x, h, k)] = feat[...]
    lower, upper = pl.ds(0, HALF), pl.ds(HALF, HALF)

    def whole(i, device):
        return go(fall.at[i], fall.at[i], device)

    def part(i, rows, device):
        return go(fall.at[i, rows], fall.at[i, rows], device)

    right, left = at("x", xo(1)), at("x", xo(3))
    own, far = place(x, h, k), place(x, 1 - h, k)
    crossed = []
    to_far = whole(own, partner)
    a_r, a_l = whole(own, right), whole(own, left)
    crossed.append(whole(own, other))
    a_r.wait_recv()
    a_rr = part(place(xo(3), h, k), lower, right)
    crossed.append(whole(place(xo(3), h, k), other))
    a_l.wait_recv()
    a_ll = part(place(xo(1), h, k), upper, left)
    crossed.append(whole(place(xo(1), h, k), other))
    to_far.wait_recv()
    b_r, b_l = whole(far, right), whole(far, left)
    crossed.append(whole(far, other))
    a_rr.wait_recv()
    a_ll.wait_recv()
    crossed.append(whole(place(xo(2), h, k), other))
    b_r.wait_recv()
    b_rr = part(place(xo(3), 1 - h, k), lower, right)
    crossed.append(whole(place(xo(3), 1 - h, k), other))
    b_l.wait_recv()
    b_ll = part(place(xo(1), 1 - h, k), upper, left)
    crossed.append(whole(place(xo(1), 1 - h, k), other))
    b_rr.wait_recv()
    b_ll.wait_recv()
    crossed.append(whole(place(xo(2), 1 - h, k), other))
    for c in crossed:
        c.wait_recv()

    hist[SLOTS] = jnp.zeros((B, F), F32)
    step = 2

    def products(source, index, before, contract):
        def one(g, carry):
            made = []
            for u in range(step):
                s = g * step + u
                made.append(
                    lax.dot_general(
                        blocks[s],
                        source[tab[index + s]],
                        (((contract,), (0,)), ((), ())),
                        preferred_element_type=F32,
                    )
                )
            for u in range(step):
                s = g * step + u
                hist[s] = made[u] + hist[tab[before + s]]
            return carry

        lax.fori_loop(0, SLOTS // step, one, 0)

    products(fall, FC, FP, 1)

    up, down = at("z", zo(1)), at("z", zo(7))
    ways = ((0, up), (1, down))
    z_ids = ids(32)

    def z_copy(n, w, device, t):
        sem = z_ids + n * 8 + w * 4 + t
        if n == 0:
            return copy(zs1.at[w, t], zr1.at[w, t], device, sem)
        return copy(zs.at[w, n - 1, t], zr.at[w, n - 1, t], device, sem)

    def row_sum(r):
        return tab[FL + r]

    for n in range(4):

        def one(t, carry, n=n):
            q = yo(1 + t)
            for w, device in ways:
                slot = row_sum(q * NZ + zo(4 - n if w == 0 else 4 + n))
                if n == 0:
                    zs1[w, t] = hist[slot, w * HALF : (w + 1) * HALF].astype(BF16)
                elif n == 1:
                    z_copy(0, w, device, t).wait_recv()
                    rows, rest = (slice(0, HALF), slice(HALF, B)) if w == 0 else (slice(HALF, B), slice(0, HALF))
                    zs[w, 0, t, rows] = (hist[slot, rows] + zr1[w, t].astype(F32)).astype(BF16)
                    zs[w, 0, t, rest] = hist[slot, rest].astype(BF16)
                else:
                    z_copy(n - 1, w, device, t).wait_recv()
                    zs[w, n - 1, t] = (hist[slot] + zr[w, n - 2, t].astype(F32)).astype(BF16)
                z_copy(n, w, device, t).start()
            return carry

        lax.fori_loop(0, NY, one, 0)

    y_copies = []
    for t in range(NY):
        for w, device in ways:
            z_copy(3, w, device, t).wait_recv()
        total = hist[row_sum(yo(1 + t) * NZ + z)] + zr[0, 2, t].astype(F32) + zr[1, 2, t].astype(F32)
        if t < NY - 1:
            ys[t] = total.astype(BF16)
            y_copies.append(go(ys.at[t], yr.at[t], at("y", yo(1 + t))))
        else:
            sown[...] = total
    for c in y_copies:
        c.wait_recv()
    agg[...] = (
        sown[...] + yr[0].astype(F32) + yr[1].astype(F32) + yr[2].astype(F32)
    ).astype(BF16)

    pre = jnp.dot(agg[...], weight[...], preferred_element_type=F32) + bias[...]
    sigma = jax.nn.sigmoid(pre)
    act_out[...] = (pre * sigma).astype(BF16)
    grad_pre = (cot[...].astype(F32) * sigma * (1.0 + pre * (1.0 - sigma))).astype(BF16)
    mine = y * NZ + z
    mid[mine] = lax.dot_general(
        grad_pre, weight[...], (((1,), (1,)), ((), ())), preferred_element_type=F32
    ).astype(BF16)

    m_ids = ids(32)

    def m_copy(n, w, device, t):
        row = yo(NY - t) * NZ + zo(NZ - n if w == 0 else n)
        sem = m_ids + n * 8 + w * 4 + t
        ref = mid.at[row]
        if n == 3:
            ref = mid.at[row, pl.ds(w * HALF, HALF)]
        return copy(ref, ref, device, sem)

    for w, device in ways:
        m_copy(0, w, device, 0).start()
    y_copies = [go(mid.at[mine], mid.at[mine], at("y", yo(t))) for t in range(1, NY)]
    for t in range(1, NY):
        y_copies[t - 1].wait_recv()
        for w, device in ways:
            m_copy(0, w, device, t).start()

    def forward_step(n):
        def one(t, carry):
            for w, device in ways:
                m_copy(n - 1, w, device, t).wait_recv()
                m_copy(n, w, device, t).start()
            return carry

        lax.fori_loop(0, NY, one, 0)

    gb = jnp.sum(grad_pre.astype(F32), axis=0, keepdims=True)
    bias_rows = jnp.broadcast_to(gb, (8, F))
    for kk in range(NK):
        g0[kk, 0:256] = lax.dot_general(
            agg[:, kk * 256 : (kk + 1) * 256], grad_pre, (((0,), (0,)), ((), ())), preferred_element_type=F32
        )
        g0[kk, 256:264] = bias_rows
    k_copy = go(g0.at[1 - k], gk, other)

    forward_step(1)

    k_copy.wait_recv()
    for xx in range(NX):
        gx[xx, 0:64] = g0[k, xx * 64 : (xx + 1) * 64] + gk[xx * 64 : (xx + 1) * 64]
        gx[xx, 64:72] = g0[k, 256:264] + gk[256:264]
    gxr[x] = gx[x]
    x_copies = [go(gx.at[xo(d)], gxr.at[x], at("x", xo(d))) for d in range(1, NX)]

    forward_step(2)

    for c in x_copies:
        c.wait_recv()
    for zz in range(NZ):
        gz[zz, 0:8] = sum(gxr[i, zz * 8 : (zz + 1) * 8] for i in range(1, NX)) + gxr[0, zz * 8 : (zz + 1) * 8]
        gz[zz, 8:16] = sum(gxr[i, 64:72] for i in range(1, NX)) + gxr[0, 64:72]
    gzr[z] = gz[z]
    zg_copies = [go(gz.at[zo(d)], gzr.at[z], at("z", zo(d))) for d in range(1, NZ)]

    forward_step(3)

    for c in zg_copies:
        c.wait_recv()
    gy[...] = sum(gzr[i] for i in range(1, NZ)) + gzr[0]
    gyr[hy] = gy[...]
    yg_copies = [go(gy, gyr.at[hy], y8(d)) for d in range(1, NH * NY)]

    def last_wait(t, carry):
        for w, device in ways:
            m_copy(3, w, device, t).wait_recv()
        return carry

    lax.fori_loop(0, NY, last_wait, 0)

    for c in yg_copies:
        c.wait_recv()
    g_total = sum(gyr[i] for i in range(1, NH * NY)) + gyr[0]
    gb_out[...] = g_total[8:9]
    gall[k, x, z] = g_total[0:8]
    zg_copies = [go(gall.at[k, x, z], gall.at[k, x, z], at("z", zo(d))) for d in range(1, NZ)]

    products(mid, BR, BP, 0)

    turns = [(1, 2), (0, 2), (1, 1), (1, 3), (0, 1), (0, 3), (1, 0), (0, 0)]

    def hp(dh):
        return 1 - h if dh else h

    k_copies = {}
    for j, (dh, dx) in enumerate(turns):
        ks[j] = hist[tab[BL + place(xo(dx), hp(dh), 1 - k)]].astype(BF16)
        k_copies[j] = go(ks.at[j], kr.at[j], other)

    for c in zg_copies:
        c.wait_recv()
    x_copies = [go(gall.at[k, x], gall.at[k, x], at("x", xo(d))) for d in range(1, NX)]

    first, second, h_copy = {}, {}, None
    for j, (dh, dx) in enumerate(turns):
        k_copies[j].wait_recv()
        slot = tab[BL + place(xo(dx), hp(dh), k)]
        if dx == 2:
            for w, device in ((0, right), (1, left)):
                rows = slice(w * HALF, (w + 1) * HALF)
                xs1[dh, w] = (hist[slot, rows] + kr[j, rows].astype(F32)).astype(BF16)
                first[dh, w] = go(xs1.at[dh, w], xr1.at[dh, w], device)
        elif dx in (1, 3):
            w = 0 if dx == 1 else 1
            first[dh, w].wait_recv()
            rows = slice(w * HALF, (w + 1) * HALF)
            rest = slice((1 - w) * HALF, (2 - w) * HALF)
            xs2[dh, w, rows] = (hist[slot, rows] + kr[j, rows].astype(F32) + xr1[dh, w].astype(F32)).astype(BF16)
            xs2[dh, w, rest] = (hist[slot, rest] + kr[j, rest].astype(F32)).astype(BF16)
            second[dh, w] = go(xs2.at[dh, w], xr2.at[dh, w], right if w == 0 else left)
        else:
            for w in (0, 1):
                second[dh, w].wait_recv()
            total = hist[slot] + kr[j].astype(F32) + xr2[dh, 0].astype(F32) + xr2[dh, 1].astype(F32)
            if dh:
                hs[...] = total.astype(BF16)
                h_copy = go(hs, hr, partner)
            else:
                sown[...] = total

    for c in x_copies:
        c.wait_recv()
    k_copy = go(gall.at[k], gall.at[k], other)

    h_copy.wait_recv()
    gin_out[...] = (sown[...] + hr[...].astype(F32)).astype(BF16)

    k_copy.wait_recv()
    gw_out[...] = gall[...].reshape(F, F)

    def sent(t, carry):
        for n in range(4):
            for w, device in ways:
                z_copy(n, w, device, t).wait_send()
                m_copy(n, w, device, t).wait_send()
        return carry

    lax.fori_loop(0, NY, sent, 0)
    for c in pending:
        c.wait_send()
    assert used[0] <= SEMS


SEMS = 176


def on_device(features, blocks, positions, counts, weight, bias, cotangent):
    smem = pl.BlockSpec(memory_space=pltpu.SMEM)
    vmem = pl.BlockSpec(memory_space=pltpu.VMEM)
    table = pl.pallas_call(
        link_slots,
        out_shape=jax.ShapeDtypeStruct((TABLE,), jnp.int32),
        in_specs=[smem, smem],
        out_specs=smem,
    )(positions.reshape(SLOTS), counts.reshape(1))
    blk = lambda *lead, rows=B, dtype=BF16: pltpu.VMEM((*lead, rows, F), dtype)
    act, gw, gb, gin = pl.pallas_call(
        layer,
        out_shape=[
            jax.ShapeDtypeStruct((B, F), BF16),
            jax.ShapeDtypeStruct((F, F), F32),
            jax.ShapeDtypeStruct((1, F), F32),
            jax.ShapeDtypeStruct((B, F), BF16),
        ],
        in_specs=[smem] + [vmem] * 5,
        out_specs=[vmem] * 4,
        scratch_shapes=[
            blk(TC),
            blk(SLOTS + 1, dtype=F32),
            blk(2, NY, rows=HALF),
            blk(2, NY, rows=HALF),
            blk(2, 3, NY),
            blk(2, 3, NY),
            blk(3),
            blk(3),
            blk(dtype=F32),
            blk(),
            blk(TR),
            blk(8),
            blk(8),
            blk(2, 2, rows=HALF),
            blk(2, 2, rows=HALF),
            blk(2, 2),
            blk(2, 2),
            blk(),
            blk(),
            blk(NK, rows=264, dtype=F32),
            blk(rows=264, dtype=F32),
            blk(NX, rows=72, dtype=F32),
            blk(NX, rows=72, dtype=F32),
            blk(NZ, rows=16, dtype=F32),
            blk(NZ, rows=16, dtype=F32),
            blk(rows=16, dtype=F32),
            blk(NH * NY, rows=16, dtype=F32),
            blk(NK, NX, NZ, rows=8, dtype=F32),
            pltpu.SemaphoreType.DMA((SEMS,)),
            pltpu.SemaphoreType.DMA((SEMS,)),
        ],
        compiler_params=pltpu.CompilerParams(
            collective_id=0, has_side_effects=True, vmem_limit_bytes=56 * 2**20
        ),
    )(table, features, blocks.reshape(SLOTS, B, B), weight, bias.reshape(1, F), cotangent)
    return act, gw, gb.reshape(F), gin


def solution(mesh):
    torus = Mesh(mesh.devices.reshape(NX, NH, NK, NY, NZ), AXES)
    return jax.shard_map(
        on_device,
        mesh=torus,
        in_specs=(
            P(COL_ROW, None),
            P(ROW, COL, None, None, None),
            P(ROW, COL, None),
            P(ROW, COL),
            P(),
            P(),
            P(ROW_COL, None),
        ),
        out_specs=(P(ROW_COL, None), P(), P(), P(COL_ROW, None)),
        check_vma=False,
    )
```

```python
import jax
import jax.numpy as jnp
from jax import lax
from jax.experimental import pallas as pl
from jax.experimental.pallas import tpu as pltpu
from jax.sharding import Mesh
from jax.sharding import PartitionSpec as P

AXES = ("x", "h", "k", "y", "z")
ROW = ("x", "h", "k")
COL = ("y", "z")
ROW_COL = ROW + COL
COL_ROW = COL + ROW
MESH = pl.DeviceIdType.MESH
NX, NH, NK, NY, NZ = 4, 2, 2, 4, 8
TR, TC = NY * NZ, NX * NH * NK
SLOTS = 48
B = 128
HALF = B // 2
F = 512
FC, FP, FL = 0, SLOTS, 2 * SLOTS
BR, BP, BL = FL + TR, FL + TR + SLOTS, FL + TR + 2 * SLOTS
TABLE = BL + TC
BF16, F32 = jnp.bfloat16, jnp.float32


def link_slots(pos, cnt, tab):
    limit = cnt[0]
    for r in range(TR):
        tab[FL + r] = SLOTS
    for c in range(TC):
        tab[BL + c] = SLOTS

    def one(s, carry):
        p = pos[s]
        r, c = lax.div(p, TC), lax.rem(p, TC)
        live = s < limit
        last_r, last_c = tab[FL + r], tab[BL + c]
        tab[FC + s] = c
        tab[BR + s] = r
        tab[FP + s] = last_r
        tab[BP + s] = last_c
        tab[FL + r] = jnp.where(live, s, last_r)
        tab[BL + c] = jnp.where(live, s, last_c)
        return carry

    lax.fori_loop(0, SLOTS, one, 0)


def layer(
    tab, feat, blocks_hbm, weight, bias, cot,
    act_out, gw_out, gb_out, gin_out,
    blocks, fall_0, fall_1, hist, zs1, zr1, zs, zr, ys, yr, own_sum, agg, mid_0, mid_1, ks, kr, xs, xr, hs, hr,
    g0, gk, gx, gxr, gy, gyr, gz, gzr, gall,
    send, recv, fetched,
):
    x, h, k, y, z = (lax.axis_index(a) for a in AXES)
    fall, mid = (fall_0, fall_1), (mid_0, mid_1)
    fetch = pltpu.make_async_copy(blocks_hbm, blocks, fetched)
    fetch.start()

    def at(name, value):
        return {name: value}

    def xo(d):
        return lax.rem(x + d, NX)

    def zo(d):
        return lax.rem(z + d, NZ)

    def yo(d):
        return lax.rem(y + d, NY)

    hy = h * NY + y

    def y8(d):
        place = lax.rem(hy + d, NH * NY)
        return {"h": lax.div(place, NY), "y": lax.rem(place, NY)}

    other = at("k", 1 - k)
    partner = at("h", 1 - h)
    up, down = at("z", zo(1)), at("z", zo(7))
    ways = ((0, up), (1, down))
    chunks = range(CHUNKS)
    cols = [slice(c * W, (c + 1) * W) for c in chunks]

    barrier = pltpu.get_barrier_semaphore()
    greeted = [other]
    greeted += [at("x", xo(d)) for d in range(1, NX)]
    greeted += [at("z", zo(d)) for d in range(1, NZ)]
    greeted += [y8(d) for d in range(1, NH * NY)]
    for device in greeted:
        pl.semaphore_signal(barrier, inc=1, device_id=device, device_id_type=MESH)

    def place(xx, hh, kk):
        return xx * (NH * NK) + hh * NK + kk

    own, far = place(x, h, k), place(x, 1 - h, k)
    for c in chunks:
        fall[c][own] = feat[:, cols[c]]
        hist[c, SLOTS] = jnp.zeros((B, W), F32)
    pl.semaphore_wait(barrier, len(greeted))

    used = [0]
    pending = []

    def ids(count):
        first = used[0]
        used[0] += count
        return first

    def copy(src, dst, device, n):
        return pltpu.make_async_remote_copy(
            src_ref=src, dst_ref=dst, send_sem=send.at[n], recv_sem=recv.at[n], device_id=device, device_id_type=MESH
        )

    def go(src, dst, device):
        c = copy(src, dst, device, ids(1))
        c.start()
        pending.append(c)
        return c

    def received(copies):
        for c in copies:
            c.wait_recv()

    def features(c):
        def whole(i, device):
            return go(fall[c].at[i], fall[c].at[i], device)

        to_far = whole(own, partner)
        own_x = [whole(own, at("x", xo(d))) for d in TURNS]
        crossed = [whole(own, other)]
        yield
        to_far.wait_recv()
        far_x = [whole(far, at("x", xo(d))) for d in TURNS]
        crossed.append(whole(far, other))
        yield
        for d, c_x in zip(TURNS, own_x):
            c_x.wait_recv()
            crossed.append(whole(place(xo(NX - d), h, k), other))
        yield
        for d, c_x in zip(TURNS, far_x):
            c_x.wait_recv()
            crossed.append(whole(place(xo(NX - d), 1 - h, k), other))
        yield
        received(crossed)
        yield

    step = 8

    def products(c, source, index, before, contract):
        def one(g, carry):
            made = []
            for u in range(step):
                s = g * step + u
                made.append(
                    lax.dot_general(
                        blocks[s],
                        source[c][tab[index + s]],
                        (((contract,), (0,)), ((), ())),
                        preferred_element_type=F32,
                    )
                )
            for u in range(step):
                s = g * step + u
                hist[c, s] = made[u] + hist[c, tab[before + s]]
            return carry

        lax.fori_loop(0, SLOTS // step, one, 0)

    z_ids = ids(32 * CHUNKS)

    def z_copy(n, c, w, device, t):
        sem = z_ids + ((c * 4 + n) * 2 + w) * NY + t
        if n == 0:
            return copy(zs1.at[c, w, t], zr1.at[c, w, t], device, sem)
        return copy(zs.at[c, w, n - 1, t], zr.at[c, w, n - 1, t], device, sem)

    def scatter_step(n, c):
        def one(t, carry):
            q = yo(1 + t)
            for w, device in ways:
                slot = tab[FL + q * NZ + zo(4 - n if w == 0 else 4 + n)]
                if n == 0:
                    zs1[c, w, t] = hist[c, slot, w * HALF : (w + 1) * HALF].astype(BF16)
                elif n == 1:
                    z_copy(0, c, w, device, t).wait_recv()
                    rows, rest = (slice(0, HALF), slice(HALF, B)) if w == 0 else (slice(HALF, B), slice(0, HALF))
                    zs[c, w, 0, t, rows] = (hist[c, slot, rows] + zr1[c, w, t].astype(F32)).astype(BF16)
                    zs[c, w, 0, t, rest] = hist[c, slot, rest].astype(BF16)
                else:
                    z_copy(n - 1, c, w, device, t).wait_recv()
                    zs[c, w, n - 1, t] = (hist[c, slot] + zr[c, w, n - 2, t].astype(F32)).astype(BF16)
                z_copy(n, c, w, device, t).start()
            return carry

        lax.fori_loop(0, NY, one, 0)

    y_copies = []

    def scatter_y(c):
        for t in range(NY):
            for w, device in ways:
                z_copy(3, c, w, device, t).wait_recv()
            slot = tab[FL + yo(1 + t) * NZ + z]
            total = hist[c, slot] + zr[c, 0, 2, t].astype(F32) + zr[c, 1, 2, t].astype(F32)
            if t < NY - 1:
                ys[c, t] = total.astype(BF16)
                y_copies.append(go(ys.at[c, t], yr.at[c, t], at("y", yo(1 + t))))
            else:
                own_sum[c] = total

    first, later = (features(c) for c in chunks)
    next(first)
    next(first)
    next(later)
    next(first)
    next(first)
    next(first)
    fetch.wait()
    products(0, fall, FC, FP, 1)
    scatter_step(0, 0)
    next(later)
    scatter_step(1, 0)
    next(later)
    next(later)
    scatter_step(2, 0)
    next(later)
    products(1, fall, FC, FP, 1)
    scatter_step(0, 1)
    scatter_step(3, 0)
    scatter_step(1, 1)
    scatter_y(0)
    scatter_step(2, 1)
    scatter_step(3, 1)
    scatter_y(1)
    received(y_copies)
    for c in chunks:
        agg[:, cols[c]] = (
            own_sum[c] + yr[c, 0].astype(F32) + yr[c, 1].astype(F32) + yr[c, 2].astype(F32)
        ).astype(BF16)

    pre = jnp.dot(agg[...], weight[...], preferred_element_type=F32) + bias[...]
    sigma = jax.nn.sigmoid(pre)
    act_out[...] = (pre * sigma).astype(BF16)
    grad_pre = (cot[...].astype(F32) * sigma * (1.0 + pre * (1.0 - sigma))).astype(BF16)
    mine = y * NZ + z
    m_ids = ids(32 * CHUNKS)

    def m_copy(n, c, w, device, t):
        row = yo(NY - t) * NZ + zo(NZ - n if w == 0 else n)
        sem = m_ids + ((c * 4 + n) * 2 + w) * NY + t
        ref = mid[c].at[row]
        if n == 3:
            ref = mid[c].at[row, pl.ds(w * HALF, HALF)]
        return copy(ref, ref, device, sem)

    m_y = []
    for c in chunks:
        mid[c][mine] = lax.dot_general(
            grad_pre, weight[cols[c], :], (((1,), (1,)), ((), ())), preferred_element_type=F32
        ).astype(BF16)
        if c == 0:
            for w, device in ways:
                m_copy(0, c, w, device, 0).start()
        m_y.append([go(mid[c].at[mine], mid[c].at[mine], at("y", yo(t))) for t in range(1, NY)])

    def gather_first(c):
        if c > 0:
            for w, device in ways:
                m_copy(0, c, w, device, 0).start()
        for t in range(1, NY):
            m_y[c][t - 1].wait_recv()
            for w, device in ways:
                m_copy(0, c, w, device, t).start()

    def gather_step(n, c):
        def one(t, carry):
            for w, device in ways:
                m_copy(n - 1, c, w, device, t).wait_recv()
                m_copy(n, c, w, device, t).start()
            return carry

        lax.fori_loop(0, NY, one, 0)

    def gather_last(c):
        def one(t, carry):
            for w, device in ways:
                m_copy(3, c, w, device, t).wait_recv()
            return carry

        lax.fori_loop(0, NY, one, 0)

    def gradients():
        gb = jnp.sum(grad_pre.astype(F32), axis=0, keepdims=True)
        bias_rows = jnp.broadcast_to(gb, (8, F))
        for kk in range(NK):
            g0[kk, 0:256] = lax.dot_general(
                agg[:, kk * 256 : (kk + 1) * 256], grad_pre, (((0,), (0,)), ((), ())), preferred_element_type=F32
            )
            g0[kk, 256:264] = bias_rows
        k_copy = go(g0.at[1 - k], gk, other)
        yield
        k_copy.wait_recv()
        for i in range(NX):
            gx[i, 0:64] = g0[k, i * 64 : (i + 1) * 64] + gk[i * 64 : (i + 1) * 64]
            gx[i, 64:72] = g0[k, 256:264] + gk[256:264]
        gxr[x] = gx[x]
        copies = [go(gx.at[xo(d)], gxr.at[x], at("x", xo(d))) for d in range(1, NX)]
        yield
        received(copies)
        bias_sum = gxr[0, 64:72] + gxr[1, 64:72] + gxr[2, 64:72] + gxr[3, 64:72]
        for i in range(NH * NY):
            rows = slice(i * 8, (i + 1) * 8)
            gy[i, 0:8] = gxr[0, rows] + gxr[1, rows] + gxr[2, rows] + gxr[3, rows]
            gy[i, 8:16] = bias_sum
        gyr[hy] = gy[hy]
        copies = [go(gy.at[lax.rem(hy + d, NH * NY)], gyr.at[hy], y8(d)) for d in range(1, NH * NY)]
        yield
        received(copies)
        total = gyr[0]
        for i in range(1, NH * NY):
            total += gyr[i]
        gz[...] = total.astype(BF16)
        gzr[z] = gz[...]
        copies = [go(gz, gzr.at[z], at("z", zo(d))) for d in range(1, NZ)]
        yield
        received(copies)
        total = gzr[0].astype(F32)
        for i in range(1, NZ):
            total += gzr[i].astype(F32)
        gb_out[...] = total[8:9]
        gall[k, x, hy] = total[0:8]
        copies = [go(gall.at[k, x, hy], gall.at[k, x, hy], y8(d)) for d in range(1, NH * NY)]
        yield
        received(copies)
        copies = [go(gall.at[k, x], gall.at[k, x], at("x", xo(d))) for d in range(1, NX)]
        yield
        received(copies)
        k_copy = go(gall.at[k], gall.at[k], other)
        yield
        k_copy.wait_recv()
        gw_out[...] = gall[...].reshape(F, F)
        yield

    def hp(dh):
        return 1 - h if dh else h

    turns = [(dh, dx) for dh in (1, 0) for dx in (*TURNS, 0)]

    def back(c):
        k_copies = []
        for j, (dh, dx) in enumerate(turns):
            ks[c, j] = hist[c, tab[BL + place(xo(dx), hp(dh), 1 - k)]].astype(BF16)
            k_copies.append(go(ks.at[c, j], kr.at[c, j], other))
        yield

        def term(j):
            dh, dx = turns[j]
            return hist[c, tab[BL + place(xo(dx), hp(dh), k)]] + kr[c, j].astype(F32)

        x_copies = {0: [], 1: []}
        for j, (dh, dx) in enumerate(turns):
            k_copies[j].wait_recv()
            if dx:
                xs[c, dh, dx - 1] = term(j).astype(BF16)
                x_copies[dh].append(go(xs.at[c, dh, dx - 1], xr.at[c, dh, dx - 1], at("x", xo(dx))))
        yield
        for dh in (1, 0):
            received(x_copies[dh])
            total = term(turns.index((dh, 0)))
            for i in range(NX - 1):
                total += xr[c, dh, i].astype(F32)
            if dh:
                hs[c] = total.astype(BF16)
                h_copy = go(hs.at[c], hr.at[c], partner)
            else:
                own_sum[c] = total
        yield
        h_copy.wait_recv()
        gin_out[:, cols[c]] = (own_sum[c] + hr[c].astype(F32)).astype(BF16)
        yield

    grads = gradients()
    backs = [back(c) for c in chunks]
    gather_first(0)
    next(grads)
    gather_step(1, 0)
    next(grads)
    gather_step(2, 0)
    gather_first(1)
    gather_step(3, 0)
    next(grads)
    gather_step(1, 1)
    gather_last(0)
    products(0, mid, BR, BP, 0)
    next(backs[0])
    gather_step(2, 1)
    next(backs[0])
    next(grads)
    gather_step(3, 1)
    next(backs[0])
    next(grads)
    gather_last(1)
    products(1, mid, BR, BP, 0)
    next(backs[1])
    next(backs[0])
    next(grads)
    next(backs[1])
    next(grads)
    next(backs[1])
    next(backs[1])
    next(grads)

    def sent(t, carry):
        for c in chunks:
            for n in range(4):
                for w, device in ways:
                    z_copy(n, c, w, device, t).wait_send()
                    m_copy(n, c, w, device, t).wait_send()
        return carry

    lax.fori_loop(0, NY, sent, 0)
    for c in pending:
        c.wait_send()
    assert used[0] <= SEMS


CHUNKS = 2
TURNS = (1, 3, 2)
W = F // CHUNKS
SEMS = 256


def hand_over(*refs):
    for source, target in zip(refs[: len(refs) // 2], refs[len(refs) // 2 :]):
        target[...] = source[...]


def on_device(features, blocks, positions, counts, weight, bias, cotangent):
    smem = pl.BlockSpec(memory_space=pltpu.SMEM)
    vmem = pl.BlockSpec(memory_space=pltpu.VMEM)
    table = pl.pallas_call(
        link_slots,
        out_shape=jax.ShapeDtypeStruct((TABLE,), jnp.int32),
        in_specs=[smem, smem],
        out_specs=smem,
    )(positions.reshape(SLOTS), counts.reshape(1))

    def chunk(*lead, rows=B, dtype=BF16):
        return pltpu.VMEM((CHUNKS, *lead, rows, W), dtype)

    def part(*lead):
        return pltpu.VMEM((*lead, B, W), BF16)

    def full(*lead, rows, dtype=F32):
        return pltpu.VMEM((*lead, rows, F), dtype)

    outs = [
        jax.ShapeDtypeStruct((B, F), BF16),
        jax.ShapeDtypeStruct((F, F), F32),
        jax.ShapeDtypeStruct((1, F), F32),
        jax.ShapeDtypeStruct((B, F), BF16),
    ]
    results = pl.pallas_call(
        layer,
        out_shape=outs,
        in_specs=[smem, vmem, pl.BlockSpec(memory_space=pl.ANY), vmem, vmem, vmem],
        out_specs=[vmem] * 4,
        scratch_shapes=[
            pltpu.VMEM((SLOTS, B, B), BF16),
            part(TC),
            part(TC),
            chunk(SLOTS + 1, dtype=F32),
            chunk(2, NY, rows=HALF),
            chunk(2, NY, rows=HALF),
            chunk(2, 3, NY),
            chunk(2, 3, NY),
            chunk(3),
            chunk(3),
            chunk(dtype=F32),
            full(rows=B, dtype=BF16),
            part(TR),
            part(TR),
            chunk(8),
            chunk(8),
            chunk(2, 3),
            chunk(2, 3),
            chunk(),
            chunk(),
            full(NK, rows=264),
            full(rows=264),
            full(NX, rows=72),
            full(NX, rows=72),
            full(NH * NY, rows=16),
            full(NH * NY, rows=16),
            full(rows=16, dtype=BF16),
            full(NZ, rows=16, dtype=BF16),
            full(NK, NX, NH * NY, rows=8),
            pltpu.SemaphoreType.DMA((SEMS,)),
            pltpu.SemaphoreType.DMA((SEMS,)),
            pltpu.SemaphoreType.DMA,
        ],
        compiler_params=pltpu.CompilerParams(
            collective_id=0, has_side_effects=True, vmem_limit_bytes=56 * 2**20
        ),
    )(table, features, blocks.reshape(SLOTS, B, B), weight, bias.reshape(1, F), cotangent)
    act, gw, gb, gin = pl.pallas_call(hand_over, out_shape=outs, in_specs=[vmem] * 4, out_specs=[vmem] * 4)(*results)
    return act, gw, gb.reshape(F), gin


def solution(mesh):
    torus = Mesh(mesh.devices.reshape(NX, NH, NK, NY, NZ), AXES)
    return jax.shard_map(
        on_device,
        mesh=torus,
        in_specs=(
            P(COL_ROW, None),
            P(ROW, COL, None, None, None),
            P(ROW, COL, None),
            P(ROW, COL),
            P(),
            P(),
            P(ROW_COL, None),
        ),
        out_specs=(P(ROW_COL, None), P(), P(), P(COL_ROW, None)),
        check_vma=False,
    )
```

```python
import jax
import jax.numpy as jnp
from jax import lax
from jax.experimental import pallas as pl
from jax.experimental.pallas import tpu as pltpu
from jax.sharding import Mesh
from jax.sharding import PartitionSpec as P

AXES = ("x", "h", "k", "y", "z")
ROW = ("x", "h", "k")
COL = ("y", "z")
ROW_COL = ROW + COL
COL_ROW = COL + ROW
MESH = pl.DeviceIdType.MESH
NX, NH, NK, NY, NZ = 4, 2, 2, 4, 8
TR, TC = NY * NZ, NX * NH * NK
SLOTS = 48
B = 128
HALF = B // 2
F = 512
FC, FP, FL = 0, SLOTS, 2 * SLOTS
BR, BP, BL = FL + TR, FL + TR + SLOTS, FL + TR + 2 * SLOTS
TABLE = BL + TC
BF16, F32 = jnp.bfloat16, jnp.float32


def link_slots(pos, cnt, tab):
    limit = cnt[0]
    for r in range(TR):
        tab[FL + r] = SLOTS
    for c in range(TC):
        tab[BL + c] = SLOTS

    def one(s, carry):
        p = pos[s]
        r, c = lax.div(p, TC), lax.rem(p, TC)
        live = s < limit
        last_r, last_c = tab[FL + r], tab[BL + c]
        tab[FC + s] = c
        tab[BR + s] = r
        tab[FP + s] = last_r
        tab[BP + s] = last_c
        tab[FL + r] = jnp.where(live, s, last_r)
        tab[BL + c] = jnp.where(live, s, last_c)
        return carry

    lax.fori_loop(0, SLOTS, one, 0)


def layer(
    tab_hbm, feat_hbm, blocks_hbm, weight_hbm, bias_hbm, cot_hbm,
    act_hbm, gw_hbm, gb_hbm, gin_hbm,
    tab, weight, bias, cot, act_out, gb_out, gin_out, blocks, fall_0, fall_1, hist, zs1, zr1, zs, zr, ys, yr, oz, y1s, y1r, y2s1, y2r1, y2s, y2r, own_sum, agg, mid_0, mid_1, mid_y, ks, kr, xs, xr, hs, hr,
    g0, gk, gx, gxr, gy, gyr, gz, gzr, gall,
    send, recv, local,
):
    x, h, k, y, z = (lax.axis_index(a) for a in AXES)
    fall, mid = (fall_0, fall_1), (mid_0, mid_1)
    narrow, early, wide = slice(0, V), slice(V, 2 * V), slice(2 * V, F)
    z_cols, z_hist = (narrow, wide), (slice(0, V), slice(0, W))
    own = (lax.axis_index("x") * NH + lax.axis_index("h")) * NK + lax.axis_index("k")
    f_in = [pltpu.make_async_copy(feat_hbm.at[:, pl.ds(c * W, W)], fall[c].at[own], local.at[c]) for c in range(CHUNKS)]
    early_in = [pltpu.make_async_copy(tab_hbm, tab, local.at[2]), pltpu.make_async_copy(blocks_hbm, blocks, local.at[3])]
    late_in = [
        pltpu.make_async_copy(weight_hbm, weight, local.at[4]),
        pltpu.make_async_copy(bias_hbm, bias, local.at[5]),
        pltpu.make_async_copy(cot_hbm, cot, local.at[6]),
    ]
    for c in (*f_in, *early_in, *late_in):
        c.start()
    act_store = pltpu.make_async_copy(act_out, act_hbm, local.at[7])
    gb_store = pltpu.make_async_copy(gb_out, gb_hbm, local.at[8])
    gin_store = pltpu.make_async_copy(gin_out, gin_hbm, local.at[9])
    stores = []

    def store(c):
        c.start()
        stores.append(c)

    def at(name, value):
        return {name: value}

    def xo(d):
        return lax.rem(x + d, NX)

    def zo(d):
        return lax.rem(z + d, NZ)

    def yo(d):
        return lax.rem(y + d, NY)

    hy = h * NY + y

    def y8(d):
        place = lax.rem(hy + d, NH * NY)
        return {"h": lax.div(place, NY), "y": lax.rem(place, NY)}

    other = at("k", 1 - k)
    partner = at("h", 1 - h)
    up, down = at("z", zo(1)), at("z", zo(7))
    ways = ((0, up), (1, down))
    chunks = range(CHUNKS)
    cols = [slice(c * W, (c + 1) * W) for c in chunks]

    barrier = pltpu.get_barrier_semaphore()
    greeted = [other]
    greeted += [at("x", xo(d)) for d in range(1, NX)]
    greeted += [at("z", zo(d)) for d in range(1, NZ)]
    greeted += [y8(d) for d in range(1, NH * NY)]
    for device in greeted:
        pl.semaphore_signal(barrier, inc=1, device_id=device, device_id_type=MESH)

    def place(xx, hh, kk):
        return xx * (NH * NK) + hh * NK + kk

    far = place(x, 1 - h, k)
    for c in chunks:
        hist[c, SLOTS] = jnp.zeros((B, W), F32)
    for c in f_in:
        c.wait()
    pl.semaphore_wait(barrier, len(greeted))

    used = [0]
    pending = []

    def ids(count):
        first = used[0]
        used[0] += count
        return first

    def copy(src, dst, device, n):
        return pltpu.make_async_remote_copy(
            src_ref=src, dst_ref=dst, send_sem=send.at[n], recv_sem=recv.at[n], device_id=device, device_id_type=MESH
        )

    def go(src, dst, device):
        c = copy(src, dst, device, ids(1))
        c.start()
        pending.append(c)
        return c

    def received(copies):
        for c in copies:
            c.wait_recv()

    def features(c):
        def whole(i, device):
            return go(fall[c].at[i], fall[c].at[i], device)

        to_far = whole(own, partner)
        own_x = [whole(own, at("x", xo(d))) for d in TURNS]
        crossed = [whole(own, other)]
        yield
        to_far.wait_recv()
        far_x = [whole(far, at("x", xo(d))) for d in TURNS]
        crossed.append(whole(far, other))
        yield
        for d, c_x in zip(TURNS, own_x):
            c_x.wait_recv()
            crossed.append(whole(place(xo(NX - d), h, k), other))
        yield
        for d, c_x in zip(TURNS, far_x):
            c_x.wait_recv()
            crossed.append(whole(place(xo(NX - d), 1 - h, k), other))
        yield
        received(crossed)
        yield

    step = 8

    def products(c, source, index, before, contract):
        def one(g, carry):
            made = []
            for u in range(step):
                s = g * step + u
                made.append(
                    lax.dot_general(
                        blocks[s],
                        source(tab[index + s]),
                        (((contract,), (0,)), ((), ())),
                        preferred_element_type=F32,
                    )
                )
            for u in range(step):
                s = g * step + u
                hist[c, s] = made[u] + hist[c, tab[before + s]]
            return carry

        lax.fori_loop(0, SLOTS // step, one, 0)

    z_ids = ids(32 * CHUNKS)

    def z_copy(n, c, w, device, t):
        sem = z_ids + ((c * 4 + n) * 2 + w) * NY + t
        if n == 0:
            return copy(zs1[c].at[w, t], zr1[c].at[w, t], device, sem)
        return copy(zs[c].at[w, n - 1, t], zr[c].at[w, n - 1, t], device, sem)

    def term(c, row, rows=slice(0, B)):
        return hist[c, tab[FL + row], rows, z_hist[c]]

    halves = (slice(0, HALF), slice(HALF, B))

    def scatter_step(n, c):
        def one(t, carry):
            q = yo(1 + t)
            for w, device in ways:
                row = q * NZ + zo(4 - n if w == 0 else 4 + n)
                if n == 0:
                    zs1[c][w, t] = term(c, row, halves[w]).astype(BF16)
                elif n == 1:
                    z_copy(0, c, w, device, t).wait_recv()
                    zs[c][w, 0, t, halves[w]] = (term(c, row, halves[w]) + zr1[c][w, t].astype(F32)).astype(BF16)
                    zs[c][w, 0, t, halves[1 - w]] = term(c, row, halves[1 - w]).astype(BF16)
                else:
                    z_copy(n - 1, c, w, device, t).wait_recv()
                    zs[c][w, n - 1, t] = (term(c, row) + zr[c][w, n - 2, t].astype(F32)).astype(BF16)
                z_copy(n, c, w, device, t).start()
            return carry

        lax.fori_loop(0, NY, one, 0)

    y_copies = []

    def scatter_y(c):
        for t in range(NY):
            for w, device in ways:
                z_copy(3, c, w, device, t).wait_recv()
            total = term(c, yo(1 + t) * NZ + z) + zr[c][0, 2, t].astype(F32) + zr[c][1, 2, t].astype(F32)
            if t < NY - 1:
                ys[c][t] = total.astype(BF16)
                y_copies.append(go(ys[c].at[t], yr[c].at[t], at("y", yo(1 + t))))
            else:
                oz[c][...] = total

    order = (4, 3, 5, 2, 6, 1, 7, 0)
    groups = (slice(0, 1), slice(1, 3), slice(3, 5), slice(5, 7), slice(7, 8))
    early_hist = slice(V, 2 * V)
    early_y, early_z = [], {}

    def early_send():
        for group in groups:
            copies = []
            for d in range(1, NY):
                for p in range(group.start, group.stop):
                    y1s[d - 1, p] = hist[0, tab[FL + yo(d) * NZ + zo(order[p])], :, early_hist].astype(BF16)
                part = pl.ds(group.start, group.stop - group.start)
                copies.append(go(y1s.at[d - 1, part], y1r.at[d - 1, part], at("y", yo(d))))
            early_y.append(copies)

    def early_term(p, rows=slice(0, B)):
        total = hist[0, tab[FL + y * NZ + zo(order[p])], rows, early_hist]
        for d in range(NY - 1):
            total += y1r[d, p, rows].astype(F32)
        return total

    def early_step(n):
        received(early_y[n])
        for w, device in ways:
            if n == 0:
                y2s1[w] = early_term(0, halves[w]).astype(BF16)
                early_z[0, w] = go(y2s1.at[w], y2r1.at[w], device)
                continue
            early_z[n - 1, w].wait_recv()
            p = 2 * n - 1 + w
            if n == 1:
                y2s[w, 0, halves[w]] = (early_term(p, halves[w]) + y2r1[w].astype(F32)).astype(BF16)
                y2s[w, 0, halves[1 - w]] = early_term(p, halves[1 - w]).astype(BF16)
            else:
                y2s[w, n - 1] = (early_term(p) + y2r[w, n - 2].astype(F32)).astype(BF16)
            early_z[n, w] = go(y2s.at[w, n - 1], y2r.at[w, n - 1], device)

    def early_last():
        received(early_y[4])
        received([early_z[3, 0], early_z[3, 1]])
        agg[:, early] = (early_term(7) + y2r[0, 2].astype(F32) + y2r[1, 2].astype(F32)).astype(BF16)

    first, later = (features(c) for c in chunks)
    next(first)
    next(first)
    next(later)
    next(first)
    next(first)
    next(first)
    for c in early_in:
        c.wait()
    products(0, lambda i: fall[0][i], FC, FP, 1)
    scatter_step(0, 0)
    early_send()
    next(later)
    scatter_step(1, 0)
    next(later)
    next(later)
    early_step(0)
    scatter_step(2, 0)
    next(later)
    products(1, lambda i: fall[1][i], FC, FP, 1)
    scatter_step(0, 1)
    scatter_step(3, 0)
    early_step(1)
    scatter_step(1, 1)
    early_step(2)
    scatter_y(0)
    scatter_step(2, 1)
    early_step(3)
    scatter_step(3, 1)
    early_last()
    scatter_y(1)
    received(y_copies)
    for c in chunks:
        agg[:, z_cols[c]] = (
            oz[c][...] + yr[c][0].astype(F32) + yr[c][1].astype(F32) + yr[c][2].astype(F32)
        ).astype(BF16)

    for c in late_in:
        c.wait()
    pre = jnp.dot(agg[...], weight[...], preferred_element_type=F32) + bias[...]
    sigma = jax.nn.sigmoid(pre)
    act_out[...] = (pre * sigma).astype(BF16)
    store(act_store)
    grad_pre = (cot[...].astype(F32) * sigma * (1.0 + pre * (1.0 - sigma))).astype(BF16)
    mine = y * NZ + z
    m_ids = ids(32 * CHUNKS)

    def m_copy(n, c, w, device, t):
        row = yo(NY - t) * NZ + zo(NZ - n if w == 0 else n)
        sem = m_ids + ((c * 4 + n) * 2 + w) * NY + t
        ref = mid[c].at[row]
        if n == 3:
            ref = mid[c].at[row, pl.ds(w * HALF, HALF)]
        return copy(ref, ref, device, sem)

    def grad_mid(part):
        return lax.dot_general(
            grad_pre, weight[part, :], (((1,), (1,)), ((), ())), preferred_element_type=F32
        ).astype(BF16)

    m_y = {}
    e_ids = ids(8)
    e_y = []

    def e_copy(n, w, device):
        row = y * NZ + zo(NZ - n if w == 0 else n)
        ref = mid_y.at[row]
        if n == 3:
            ref = mid_y.at[row, pl.ds(w * HALF, HALF)]
        return copy(ref, ref, device, e_ids + n * 2 + w)

    def e_spread(row):
        for t in range(1, NY):
            e_y.append(go(mid_y.at[row], mid_y.at[row], at("y", yo(t))))

    def early_gather(n):
        for w, device in ways:
            if n > 0:
                e_copy(n - 1, w, device).wait_recv()
            if n < 4:
                e_copy(n, w, device).start()
        if n == 0:
            e_spread(mine)
        elif n < 4:
            e_spread(y * NZ + zo(NZ - n))
            e_spread(y * NZ + zo(n))
        else:
            e_spread(y * NZ + zo(4))

    for c in (1, 0):
        mid[c][mine] = grad_mid(z_cols[c])
        if c == 1:
            for w, device in ways:
                m_copy(0, c, w, device, 0).start()
        m_y[c] = [go(mid[c].at[mine], mid[c].at[mine], at("y", yo(t))) for t in range(1, NY)]
        if c == 1:
            mid_y[mine] = grad_mid(early)
            early_gather(0)

    def gather_first(c):
        if c == 0:
            for w, device in ways:
                m_copy(0, c, w, device, 0).start()
        for t in range(1, NY):
            m_y[c][t - 1].wait_recv()
            for w, device in ways:
                m_copy(0, c, w, device, t).start()

    def gather_step(n, c):
        def one(t, carry):
            for w, device in ways:
                m_copy(n - 1, c, w, device, t).wait_recv()
                m_copy(n, c, w, device, t).start()
            return carry

        lax.fori_loop(0, NY, one, 0)

    def gather_last(c):
        def one(t, carry):
            for w, device in ways:
                m_copy(3, c, w, device, t).wait_recv()
            return carry

        lax.fori_loop(0, NY, one, 0)

    def gradients():
        gb = jnp.sum(grad_pre.astype(F32), axis=0, keepdims=True)
        bias_rows = jnp.broadcast_to(gb, (8, F))
        for kk in range(NK):
            g0[kk, 0:256] = lax.dot_general(
                agg[:, kk * 256 : (kk + 1) * 256], grad_pre, (((0,), (0,)), ((), ())), preferred_element_type=F32
            )
            g0[kk, 256:264] = bias_rows
        k_copy = go(g0.at[1 - k], gk, other)
        yield
        k_copy.wait_recv()
        for i in range(NX):
            gx[i, 0:64] = g0[k, i * 64 : (i + 1) * 64] + gk[i * 64 : (i + 1) * 64]
            gx[i, 64:72] = g0[k, 256:264] + gk[256:264]
        gxr[x] = gx[x]
        copies = [go(gx.at[xo(d)], gxr.at[x], at("x", xo(d))) for d in range(1, NX)]
        yield
        received(copies)
        bias_sum = gxr[0, 64:72] + gxr[1, 64:72] + gxr[2, 64:72] + gxr[3, 64:72]
        for i in range(NH * NY):
            rows = slice(i * 8, (i + 1) * 8)
            gy[i, 0:8] = gxr[0, rows] + gxr[1, rows] + gxr[2, rows] + gxr[3, rows]
            gy[i, 8:16] = bias_sum
        gyr[hy] = gy[hy]
        copies = [go(gy.at[lax.rem(hy + d, NH * NY)], gyr.at[hy], y8(d)) for d in range(1, NH * NY)]
        yield
        received(copies)
        total = gyr[0]
        for i in range(1, NH * NY):
            total += gyr[i]
        gz[...] = total.astype(BF16)
        gzr[z] = gz[...]
        copies = [go(gz, gzr.at[z], at("z", zo(d))) for d in range(1, NZ)]
        yield
        received(copies)
        total = gzr[0].astype(F32)
        for i in range(1, NZ):
            total += gzr[i].astype(F32)
        gb_out[...] = total[8:9]
        store(gb_store)
        gall[k, x, hy] = total[0:8]
        copies = [go(gall.at[k, x, hy], gall.at[k, x, hy], y8(d)) for d in range(1, NH * NY)]
        yield
        received(copies)
        copies = [go(gall.at[k, x], gall.at[k, x], at("x", xo(d))) for d in range(1, NX)]
        yield
        received(copies)
        k_copy = go(gall.at[k], gall.at[k], other)
        store(pltpu.make_async_copy(gall.at[k], gw_hbm.at[k], local.at[10]))
        yield
        k_copy.wait_recv()
        store(pltpu.make_async_copy(gall.at[1 - k], gw_hbm.at[1 - k], local.at[11]))
        yield

    def hp(dh):
        return 1 - h if dh else h

    turns = [(dh, dx) for dh in (1, 0) for dx in (*TURNS, 0)]

    def back(c):
        k_copies = []
        for j, (dh, dx) in enumerate(turns):
            ks[c, j] = hist[c, tab[BL + place(xo(dx), hp(dh), 1 - k)]].astype(BF16)
            k_copies.append(go(ks.at[c, j], kr.at[c, j], other))
        yield

        def back_term(j):
            dh, dx = turns[j]
            return hist[c, tab[BL + place(xo(dx), hp(dh), k)]] + kr[c, j].astype(F32)

        def x_sends(dh):
            copies = []
            for j, (dj, dx) in enumerate(turns):
                if dj == dh:
                    k_copies[j].wait_recv()
                    if dx:
                        xs[c, dh, dx - 1] = back_term(j).astype(BF16)
                        copies.append(go(xs.at[c, dh, dx - 1], xr.at[c, dh, dx - 1], at("x", xo(dx))))
            return copies

        def x_sum(dh, copies):
            received(copies)
            total = back_term(turns.index((dh, 0)))
            for i in range(NX - 1):
                total += xr[c, dh, i].astype(F32)
            return total

        copies = x_sends(1)
        yield
        hs[c] = x_sum(1, copies).astype(BF16)
        h_copy = go(hs.at[c], hr.at[c], partner)
        copies = x_sends(0)
        yield
        own_sum[c] = x_sum(0, copies)
        yield
        h_copy.wait_recv()
        gin_out[:, cols[c]] = (own_sum[c] + hr[c].astype(F32)).astype(BF16)
        yield

    grads = gradients()
    backs = [back(c) for c in chunks]
    gather_first(1)
    next(grads)
    early_gather(1)
    gather_step(1, 1)
    next(grads)
    early_gather(2)
    gather_step(2, 1)
    early_gather(3)
    gather_step(3, 1)
    next(grads)
    gather_first(0)
    early_gather(4)
    gather_last(1)
    gather_step(1, 0)
    products(1, lambda i: mid[1][i], BR, BP, 0)
    next(backs[1])
    gather_step(2, 0)
    next(backs[1])
    next(grads)
    gather_step(3, 0)
    next(backs[1])
    next(backs[1])
    gather_last(0)
    received(e_y)
    next(grads)
    products(0, lambda i: jnp.concatenate([mid[0][i], mid_y[i]], axis=1), BR, BP, 0)
    next(backs[0])
    next(backs[1])
    next(backs[0])
    next(grads)
    next(backs[0])
    next(backs[0])
    next(grads)
    next(backs[0])
    store(gin_store)
    next(grads)
    for c in stores:
        c.wait()

    def sent(t, carry):
        for c in chunks:
            for n in range(4):
                for w, device in ways:
                    z_copy(n, c, w, device, t).wait_send()
                    m_copy(n, c, w, device, t).wait_send()
        return carry

    lax.fori_loop(0, NY, sent, 0)
    for n in range(4):
        for w, device in ways:
            e_copy(n, w, device).wait_send()
    for c in pending:
        c.wait_send()
    assert used[0] <= SEMS


CHUNKS = 2
TURNS = (1, 3, 2)
W = F // CHUNKS
V = W // 2
SEMS = 320


def hand_over(*refs):
    half = len(refs) // 2
    for source, target in zip(refs[:half], refs[half:]):
        target[...] = source[...]


def on_device(features, blocks, positions, counts, weight, bias, cotangent):
    smem = pl.BlockSpec(memory_space=pltpu.SMEM)
    anywhere = pl.BlockSpec(memory_space=pl.ANY)
    table = pl.pallas_call(
        link_slots,
        out_shape=jax.ShapeDtypeStruct((TABLE,), jnp.int32),
        in_specs=[smem, smem],
        out_specs=smem,
    )(positions.reshape(SLOTS), counts.reshape(1))

    def chunk(*lead, rows=B, dtype=BF16):
        return pltpu.VMEM((CHUNKS, *lead, rows, W), dtype)

    def part(*lead, rows=B, cols=W, dtype=BF16):
        return pltpu.VMEM((*lead, rows, cols), dtype)

    def pair(*lead, rows=B, dtype=BF16):
        return part(*lead, rows=rows, cols=V, dtype=dtype), part(*lead, rows=rows, dtype=dtype)

    def full(*lead, rows, dtype=F32):
        return pltpu.VMEM((*lead, rows, F), dtype)

    outs = [
        jax.ShapeDtypeStruct((B, F), BF16),
        jax.ShapeDtypeStruct((NK, NX, NH * NY, 8, F), F32),
        jax.ShapeDtypeStruct((1, F), F32),
        jax.ShapeDtypeStruct((B, F), BF16),
    ]
    results = pl.pallas_call(
        layer,
        out_shape=outs,
        in_specs=[anywhere] * 6,
        out_specs=[anywhere] * 4,
        scratch_shapes=[
            pltpu.SMEM((TABLE,), jnp.int32),
            pltpu.VMEM((F, F), BF16),
            pltpu.VMEM((1, F), F32),
            pltpu.VMEM((B, F), BF16),
            pltpu.VMEM((B, F), BF16),
            pltpu.VMEM((1, F), F32),
            pltpu.VMEM((B, F), BF16),
            pltpu.VMEM((SLOTS, B, B), BF16),
            part(TC),
            part(TC),
            chunk(SLOTS + 1, dtype=F32),
            pair(2, NY, rows=HALF),
            pair(2, NY, rows=HALF),
            pair(2, 3, NY),
            pair(2, 3, NY),
            pair(3),
            pair(3),
            pair(dtype=F32),
            part(3, NZ, cols=V),
            part(3, NZ, cols=V),
            part(2, rows=HALF, cols=V),
            part(2, rows=HALF, cols=V),
            part(2, 3, cols=V),
            part(2, 3, cols=V),
            chunk(dtype=F32),
            full(rows=B, dtype=BF16),
            part(TR, cols=V),
            part(TR),
            part(TR, cols=V),
            chunk(8),
            chunk(8),
            chunk(2, 3),
            chunk(2, 3),
            chunk(),
            chunk(),
            full(NK, rows=264),
            full(rows=264),
            full(NX, rows=72),
            full(NX, rows=72),
            full(NH * NY, rows=16),
            full(NH * NY, rows=16),
            full(rows=16, dtype=BF16),
            full(NZ, rows=16, dtype=BF16),
            full(NK, NX, NH * NY, rows=8),
            pltpu.SemaphoreType.DMA((SEMS,)),
            pltpu.SemaphoreType.DMA((SEMS,)),
            pltpu.SemaphoreType.DMA((12,)),
        ],
        compiler_params=pltpu.CompilerParams(
            collective_id=0, has_side_effects=True, vmem_limit_bytes=56 * 2**20
        ),
    )(table, features, blocks.reshape(SLOTS, B, B), weight, bias.reshape(1, F), cotangent)
    vmem = pl.BlockSpec(memory_space=pltpu.VMEM)
    act, gw, gb, gin = pl.pallas_call(hand_over, out_shape=outs, in_specs=[vmem] * 4, out_specs=[vmem] * 4)(*results)
    return act, gw.reshape(F, F), gb.reshape(F), gin


def solution(mesh):
    torus = Mesh(mesh.devices.reshape(NX, NH, NK, NY, NZ), AXES)
    return jax.shard_map(
        on_device,
        mesh=torus,
        in_specs=(
            P(COL_ROW, None),
            P(ROW, COL, None, None, None),
            P(ROW, COL, None),
            P(ROW, COL),
            P(),
            P(),
            P(ROW_COL, None),
        ),
        out_specs=(P(ROW_COL, None), P(), P(), P(COL_ROW, None)),
        check_vma=False,
    )
```

```python
import jax
import jax.numpy as jnp
from jax import lax
from jax.experimental import pallas as pl
from jax.experimental.pallas import tpu as pltpu
from jax.sharding import Mesh
from jax.sharding import PartitionSpec as P

AXES = ("x", "h", "k", "y", "z")
ROW = ("x", "h", "k")
COL = ("y", "z")
ROW_COL = ROW + COL
COL_ROW = COL + ROW
MESH = pl.DeviceIdType.MESH
NX, NH, NK, NY, NZ = 4, 2, 2, 4, 8
TR, TC = NY * NZ, NX * NH * NK
SLOTS = 48
B = 128
HALF = B // 2
F = 512
FC, FP, FL = 0, SLOTS, 2 * SLOTS
BR, BP, BL = FL + TR, FL + TR + SLOTS, FL + TR + 2 * SLOTS
TABLE = BL + TC
BF16, F32 = jnp.bfloat16, jnp.float32


def link_slots(pos, cnt, tab):
    limit = cnt[0]
    for r in range(TR):
        tab[FL + r] = SLOTS
    for c in range(TC):
        tab[BL + c] = SLOTS

    def one(s, carry):
        p = pos[s]
        r, c = lax.div(p, TC), lax.rem(p, TC)
        live = s < limit
        last_r, last_c = tab[FL + r], tab[BL + c]
        tab[FC + s] = c
        tab[BR + s] = r
        tab[FP + s] = last_r
        tab[BP + s] = last_c
        tab[FL + r] = jnp.where(live, s, last_r)
        tab[BL + c] = jnp.where(live, s, last_c)
        return carry

    lax.fori_loop(0, SLOTS, one, 0)


def layer(
    tab_hbm, feat_hbm, blocks_hbm, weight_hbm, bias_hbm, cot_hbm,
    act_hbm, gw_hbm, gb_hbm, gin_hbm,
    tab, weight, bias, cot, act_out, gb_out, gin_out, blocks, fall_0, fall_1, hist, zs1, zr1, zs, zr, ys, yr, oz, y1s, y1r, y2s1, y2r1, y2s, y2r, own_sum, agg, mid_0, mid_1, mid_y, ks, kr, xs, xr, hs, hr,
    g0, gk, gx, gxr, gy, gyr, gz, gzr, gall,
    send, recv, local,
):
    x, h, k, y, z = (lax.axis_index(a) for a in AXES)
    fall, mid = (fall_0, fall_1), (mid_0, mid_1)
    narrow, early, wide = slice(0, V), slice(V, 2 * V), slice(2 * V, F)
    z_cols, z_hist = (narrow, wide), (slice(0, V), slice(0, W))
    own = (lax.axis_index("x") * NH + lax.axis_index("h")) * NK + lax.axis_index("k")
    f_in = [pltpu.make_async_copy(feat_hbm.at[:, pl.ds(c * W, W)], fall[c].at[own], local.at[c]) for c in range(CHUNKS)]
    early_in = [pltpu.make_async_copy(tab_hbm, tab, local.at[2]), pltpu.make_async_copy(blocks_hbm, blocks, local.at[3])]
    late_in = [
        pltpu.make_async_copy(weight_hbm, weight, local.at[4]),
        pltpu.make_async_copy(bias_hbm, bias, local.at[5]),
        pltpu.make_async_copy(cot_hbm, cot, local.at[6]),
    ]
    for c in (*f_in, *early_in, *late_in):
        c.start()
    act_store = pltpu.make_async_copy(act_out, act_hbm, local.at[7])
    gb_store = pltpu.make_async_copy(gb_out, gb_hbm, local.at[8])
    gin_store = pltpu.make_async_copy(gin_out, gin_hbm, local.at[9])
    stores = []

    def store(c):
        c.start()
        stores.append(c)

    def at(name, value):
        return {name: value}

    def xo(d):
        return lax.rem(x + d, NX)

    def zo(d):
        return lax.rem(z + d, NZ)

    def yo(d):
        return lax.rem(y + d, NY)

    hy = h * NY + y

    def y8(d):
        place = lax.rem(hy + d, NH * NY)
        return {"h": lax.div(place, NY), "y": lax.rem(place, NY)}

    other = at("k", 1 - k)
    partner = at("h", 1 - h)
    up, down = at("z", zo(1)), at("z", zo(7))
    ways = ((0, up), (1, down))
    chunks = range(CHUNKS)
    cols = [slice(c * W, (c + 1) * W) for c in chunks]

    barrier = pltpu.get_barrier_semaphore()
    greeted = [other]
    greeted += [at("x", xo(d)) for d in range(1, NX)]
    greeted += [at("z", zo(d)) for d in range(1, NZ)]
    greeted += [y8(d) for d in range(1, NH * NY)]
    for device in greeted:
        pl.semaphore_signal(barrier, inc=1, device_id=device, device_id_type=MESH)

    def place(xx, hh, kk):
        return xx * (NH * NK) + hh * NK + kk

    far = place(x, 1 - h, k)
    for c in chunks:
        hist[c, SLOTS] = jnp.zeros((B, W), F32)
    for c in f_in:
        c.wait()
    pl.semaphore_wait(barrier, len(greeted))

    used, leaving = [0], []

    def ids(count):
        first = used[0]
        used[0] += count
        return first

    def leaves(ref):
        leaving.append(ref)
        return len(leaving) - 1

    def copy(src, dst, device, sent, n):
        return pltpu.make_async_remote_copy(
            src_ref=src, dst_ref=dst, send_sem=send.at[sent], recv_sem=recv.at[n], device_id=device, device_id_type=MESH
        )

    def go(src, dst, device, sent, n=None):
        c = copy(src, dst, device, sent, ids(1) if n is None else n)
        c.start()
        return c

    def received(copies):
        for c in copies:
            c.wait_recv()

    def together(sources, target, devices, ref):
        sent, n = leaves(ref), ids(1)
        for source, device in zip(sources, devices):
            go(source, target, device, sent, n)
        return copy(ref, ref, other, sent, n)

    def features(c):
        sent, cross = leaves(fall[c].at[pl.ds(0, 15)]), ids(1)

        def whole(i, device, n=None):
            return go(fall[c].at[i], fall[c].at[i], device, sent, n)

        to_far = whole(own, partner)
        own_x = [whole(own, at("x", xo(d))) for d in TURNS]
        whole(own, other, cross)
        yield
        to_far.wait_recv()
        far_x = [whole(far, at("x", xo(d))) for d in TURNS]
        whole(far, other, cross)
        yield
        for d, c_x in zip(TURNS, own_x):
            c_x.wait_recv()
            whole(place(xo(NX - d), h, k), other, cross)
        yield
        for d, c_x in zip(TURNS, far_x):
            c_x.wait_recv()
            whole(place(xo(NX - d), 1 - h, k), other, cross)
        yield
        eight = fall[c].at[pl.ds(0, TC // NK)]
        copy(eight, eight, other, sent, cross).wait_recv()
        yield

    step = 8

    def products(c, source, index, before, contract):
        def one(g, carry):
            made = []
            for u in range(step):
                s = g * step + u
                made.append(
                    lax.dot_general(
                        blocks[s],
                        source(tab[index + s]),
                        (((contract,), (0,)), ((), ())),
                        preferred_element_type=F32,
                    )
                )
            for u in range(step):
                s = g * step + u
                hist[c, s] = made[u] + hist[c, tab[before + s]]
            return carry

        lax.fori_loop(0, SLOTS // step, one, 0)

    z_ids = ids(32 * CHUNKS)
    z_sent = [(leaves(zs1[c]), leaves(zs[c])) for c in chunks]

    def z_copy(n, c, w, device, t):
        sem = z_ids + ((c * 4 + n) * 2 + w) * NY + t
        if n == 0:
            return copy(zs1[c].at[w, t], zr1[c].at[w, t], device, z_sent[c][0], sem)
        return copy(zs[c].at[w, n - 1, t], zr[c].at[w, n - 1, t], device, z_sent[c][1], sem)

    def term(c, row, rows=slice(0, B)):
        return hist[c, tab[FL + row], rows, z_hist[c]]

    halves = (slice(0, HALF), slice(HALF, B))

    def scatter_step(n, c):
        def one(t, carry):
            q = yo(1 + t)
            for w, device in ways:
                row = q * NZ + zo(4 - n if w == 0 else 4 + n)
                if n == 0:
                    zs1[c][w, t] = term(c, row, halves[w]).astype(BF16)
                elif n == 1:
                    z_copy(0, c, w, device, t).wait_recv()
                    zs[c][w, 0, t, halves[w]] = (term(c, row, halves[w]) + zr1[c][w, t].astype(F32)).astype(BF16)
                    zs[c][w, 0, t, halves[1 - w]] = term(c, row, halves[1 - w]).astype(BF16)
                else:
                    z_copy(n - 1, c, w, device, t).wait_recv()
                    zs[c][w, n - 1, t] = (term(c, row) + zr[c][w, n - 2, t].astype(F32)).astype(BF16)
                z_copy(n, c, w, device, t).start()
            return carry

        lax.fori_loop(0, NY, one, 0)

    y_copies = []

    def scatter_y(c):
        sent = leaves(ys[c])
        for t in range(NY):
            for w, device in ways:
                z_copy(3, c, w, device, t).wait_recv()
            total = term(c, yo(1 + t) * NZ + z) + zr[c][0, 2, t].astype(F32) + zr[c][1, 2, t].astype(F32)
            if t < NY - 1:
                ys[c][t] = total.astype(BF16)
                y_copies.append(go(ys[c].at[t], yr[c].at[t], at("y", yo(1 + t)), sent))
            else:
                oz[c][...] = total

    order = (4, 3, 5, 2, 6, 1, 7, 0)
    groups = (slice(0, 1), slice(1, 3), slice(3, 5), slice(5, 7), slice(7, 8))
    early_hist = slice(V, 2 * V)
    early_y, early_z = [], {}
    early_sent = [leaves(ref) for ref in (y1s, y2s1, y2s)]

    def early_send():
        for group in groups:
            copies = []
            for d in range(1, NY):
                for p in range(group.start, group.stop):
                    y1s[d - 1, p] = hist[0, tab[FL + yo(d) * NZ + zo(order[p])], :, early_hist].astype(BF16)
                part = pl.ds(group.start, group.stop - group.start)
                copies.append(go(y1s.at[d - 1, part], y1r.at[d - 1, part], at("y", yo(d)), early_sent[0]))
            early_y.append(copies)

    def early_term(p, rows=slice(0, B)):
        total = hist[0, tab[FL + y * NZ + zo(order[p])], rows, early_hist]
        for d in range(NY - 1):
            total += y1r[d, p, rows].astype(F32)
        return total

    def early_step(n):
        received(early_y[n])
        for w, device in ways:
            if n == 0:
                y2s1[w] = early_term(0, halves[w]).astype(BF16)
                early_z[0, w] = go(y2s1.at[w], y2r1.at[w], device, early_sent[1])
                continue
            early_z[n - 1, w].wait_recv()
            p = 2 * n - 1 + w
            if n == 1:
                y2s[w, 0, halves[w]] = (early_term(p, halves[w]) + y2r1[w].astype(F32)).astype(BF16)
                y2s[w, 0, halves[1 - w]] = early_term(p, halves[1 - w]).astype(BF16)
            else:
                y2s[w, n - 1] = (early_term(p) + y2r[w, n - 2].astype(F32)).astype(BF16)
            early_z[n, w] = go(y2s.at[w, n - 1], y2r.at[w, n - 1], device, early_sent[2])

    def early_last():
        received(early_y[4])
        received([early_z[3, 0], early_z[3, 1]])
        agg[:, early] = (early_term(7) + y2r[0, 2].astype(F32) + y2r[1, 2].astype(F32)).astype(BF16)

    first, later = (features(c) for c in chunks)
    next(first)
    next(first)
    next(later)
    next(first)
    next(first)
    next(later)
    next(first)
    for c in early_in:
        c.wait()
    products(0, lambda i: fall[0][i], FC, FP, 1)
    scatter_step(0, 0)
    early_send()
    next(later)
    scatter_step(1, 0)
    next(later)
    early_step(0)
    scatter_step(2, 0)
    next(later)
    products(1, lambda i: fall[1][i], FC, FP, 1)
    scatter_step(0, 1)
    scatter_step(3, 0)
    early_step(1)
    scatter_step(1, 1)
    early_step(2)
    scatter_y(0)
    scatter_step(2, 1)
    early_step(3)
    scatter_step(3, 1)
    early_last()
    scatter_y(1)
    received(y_copies)
    for c in chunks:
        agg[:, z_cols[c]] = (
            oz[c][...] + yr[c][0].astype(F32) + yr[c][1].astype(F32) + yr[c][2].astype(F32)
        ).astype(BF16)

    for c in late_in:
        c.wait()
    pre = jnp.dot(agg[...], weight[...], preferred_element_type=F32) + bias[...]
    sigma = jax.nn.sigmoid(pre)
    act_out[...] = (pre * sigma).astype(BF16)
    store(act_store)
    grad_pre = (cot[...].astype(F32) * sigma * (1.0 + pre * (1.0 - sigma))).astype(BF16)
    mine = y * NZ + z
    m_ids = ids(32 * CHUNKS)
    m_sent = [leaves(mid[c].at[pl.ds(0, 31)]) for c in chunks]

    def m_copy(n, c, w, device, t):
        row = yo(NY - t) * NZ + zo(NZ - n if w == 0 else n)
        sem = m_ids + ((c * 4 + n) * 2 + w) * NY + t
        ref = mid[c].at[row]
        if n == 3:
            ref = mid[c].at[row, pl.ds(w * HALF, HALF)]
        return copy(ref, ref, device, m_sent[c], sem)

    def grad_mid(part):
        return lax.dot_general(
            grad_pre, weight[part, :], (((1,), (1,)), ((), ())), preferred_element_type=F32
        ).astype(BF16)

    m_y = {}
    e_ids, e_y = ids(8), ids(1)
    e_sent = leaves(mid_y.at[pl.ds(0, 31)])

    def e_copy(n, w, device):
        row = y * NZ + zo(NZ - n if w == 0 else n)
        ref = mid_y.at[row]
        if n == 3:
            ref = mid_y.at[row, pl.ds(w * HALF, HALF)]
        return copy(ref, ref, device, e_sent, e_ids + n * 2 + w)

    def e_spread(row):
        for t in range(1, NY):
            go(mid_y.at[row], mid_y.at[row], at("y", yo(t)), e_sent, e_y)

    def early_gather(n):
        for w, device in ways:
            if n > 0:
                e_copy(n - 1, w, device).wait_recv()
            if n < 4:
                e_copy(n, w, device).start()
        if n == 0:
            e_spread(mine)
        elif n < 4:
            e_spread(y * NZ + zo(NZ - n))
            e_spread(y * NZ + zo(n))
        else:
            e_spread(y * NZ + zo(4))

    for c in (1, 0):
        mid[c][mine] = grad_mid(z_cols[c])
        if c == 1:
            for w, device in ways:
                m_copy(0, c, w, device, 0).start()
        m_y[c] = [go(mid[c].at[mine], mid[c].at[mine], at("y", yo(t)), m_sent[c]) for t in range(1, NY)]
        if c == 1:
            mid_y[mine] = grad_mid(early)
            early_gather(0)

    def gather_first(c):
        if c == 0:
            for w, device in ways:
                m_copy(0, c, w, device, 0).start()
        for t in range(1, NY):
            m_y[c][t - 1].wait_recv()
            for w, device in ways:
                m_copy(0, c, w, device, t).start()

    def gather_step(n, c):
        def one(t, carry):
            for w, device in ways:
                m_copy(n - 1, c, w, device, t).wait_recv()
                m_copy(n, c, w, device, t).start()
            return carry

        lax.fori_loop(0, NY, one, 0)

    def gather_last(c):
        def one(t, carry):
            for w, device in ways:
                m_copy(3, c, w, device, t).wait_recv()
            return carry

        lax.fori_loop(0, NY, one, 0)

    def gradients():
        gb = jnp.sum(grad_pre.astype(F32), axis=0, keepdims=True)
        bias_rows = jnp.broadcast_to(gb, (8, F))
        for kk in range(NK):
            g0[kk, 0:256] = lax.dot_general(
                agg[:, kk * 256 : (kk + 1) * 256], grad_pre, (((0,), (0,)), ((), ())), preferred_element_type=F32
            )
            g0[kk, 256:264] = bias_rows
        k_copy = go(g0.at[1 - k], gk, other, leaves(gk))
        yield
        k_copy.wait_recv()
        for i in range(NX):
            gx[i, 0:64] = g0[k, i * 64 : (i + 1) * 64] + gk[i * 64 : (i + 1) * 64]
            gx[i, 64:72] = g0[k, 256:264] + gk[256:264]
        gxr[x] = gx[x]
        x_devices = [at("x", xo(d)) for d in range(1, NX)]
        y_devices = [y8(d) for d in range(1, NH * NY)]
        copies = together([gx.at[xo(d)] for d in range(1, NX)], gxr.at[x], x_devices, gxr.at[pl.ds(0, 3)])
        yield
        copies.wait_recv()
        bias_sum = gxr[0, 64:72] + gxr[1, 64:72] + gxr[2, 64:72] + gxr[3, 64:72]
        for i in range(NH * NY):
            rows = slice(i * 8, (i + 1) * 8)
            gy[i, 0:8] = gxr[0, rows] + gxr[1, rows] + gxr[2, rows] + gxr[3, rows]
            gy[i, 8:16] = bias_sum
        gyr[hy] = gy[hy]
        sources = [gy.at[lax.rem(hy + d, NH * NY)] for d in range(1, NH * NY)]
        copies = together(sources, gyr.at[hy], y_devices, gyr.at[pl.ds(0, 7)])
        yield
        copies.wait_recv()
        total = gyr[0]
        for i in range(1, NH * NY):
            total += gyr[i]
        gz[...] = total.astype(BF16)
        gzr[z] = gz[...]
        copies = together([gz] * 7, gzr.at[z], [at("z", zo(d)) for d in range(1, NZ)], gzr.at[pl.ds(0, 7)])
        yield
        copies.wait_recv()
        total = gzr[0].astype(F32)
        for i in range(1, NZ):
            total += gzr[i].astype(F32)
        gb_out[...] = total[8:9]
        store(gb_store)
        gall[k, x, hy] = total[0:8]
        piece = gall.at[k, x, hy]
        copies = together([piece] * 7, piece, y_devices, gall.at[0, 0, pl.ds(0, 7)])
        yield
        copies.wait_recv()
        piece = gall.at[k, x]
        copies = together([piece] * 3, piece, x_devices, gall.at[0, pl.ds(0, 3)])
        yield
        copies.wait_recv()
        k_copy = go(gall.at[k], gall.at[k], other, leaves(gall.at[0]))
        store(pltpu.make_async_copy(gall.at[k], gw_hbm.at[k], local.at[10]))
        yield
        k_copy.wait_recv()
        store(pltpu.make_async_copy(gall.at[1 - k], gw_hbm.at[1 - k], local.at[11]))
        yield

    def hp(dh):
        return 1 - h if dh else h

    turns = [(dh, dx) for dh in (1, 0) for dx in (*TURNS, 0)]

    def back(c):
        sent_k, sent_x = leaves(ks.at[c]), leaves(xs.at[c])
        k_copies = []
        for j, (dh, dx) in enumerate(turns):
            ks[c, j] = hist[c, tab[BL + place(xo(dx), hp(dh), 1 - k)]].astype(BF16)
            k_copies.append(go(ks.at[c, j], kr.at[c, j], other, sent_k))
        yield

        def back_term(j):
            dh, dx = turns[j]
            return hist[c, tab[BL + place(xo(dx), hp(dh), k)]] + kr[c, j].astype(F32)

        def x_sends(dh):
            copies = []
            for j, (dj, dx) in enumerate(turns):
                if dj == dh:
                    k_copies[j].wait_recv()
                    if dx:
                        xs[c, dh, dx - 1] = back_term(j).astype(BF16)
                        copies.append(go(xs.at[c, dh, dx - 1], xr.at[c, dh, dx - 1], at("x", xo(dx)), sent_x))
            return copies

        def x_sum(dh, copies):
            received(copies)
            total = back_term(turns.index((dh, 0)))
            for i in range(NX - 1):
                total += xr[c, dh, i].astype(F32)
            return total

        copies = x_sends(1)
        yield
        hs[c] = x_sum(1, copies).astype(BF16)
        h_copy = go(hs.at[c], hr.at[c], partner, leaves(hs.at[c]))
        copies = x_sends(0)
        yield
        own_sum[c] = x_sum(0, copies)
        yield
        h_copy.wait_recv()
        gin_out[:, cols[c]] = (own_sum[c] + hr[c].astype(F32)).astype(BF16)
        yield

    grads = gradients()
    backs = [back(c) for c in chunks]
    gather_first(1)
    next(grads)
    early_gather(1)
    gather_step(1, 1)
    next(grads)
    early_gather(2)
    gather_step(2, 1)
    early_gather(3)
    gather_step(3, 1)
    next(grads)
    gather_first(0)
    early_gather(4)
    gather_last(1)
    gather_step(1, 0)
    products(1, lambda i: mid[1][i], BR, BP, 0)
    next(backs[1])
    gather_step(2, 0)
    next(backs[1])
    next(grads)
    gather_step(3, 0)
    next(backs[1])
    next(backs[1])
    gather_last(0)
    most = mid_y.at[pl.ds(0, NZ * (NY - 1))]
    copy(most, most, up, e_sent, e_y).wait_recv()
    next(grads)
    products(0, lambda i: jnp.concatenate([mid[0][i], mid_y[i]], axis=1), BR, BP, 0)
    next(backs[0])
    next(backs[1])
    next(backs[0])
    next(grads)
    next(backs[0])
    next(backs[0])
    next(grads)
    next(backs[0])
    store(gin_store)
    next(grads)
    for c in stores:
        c.wait()

    for n, ref in enumerate(leaving):
        copy(ref, ref, other, n, 0).wait_send()
    assert used[0] == ARRIVE and len(leaving) == LEAVE


CHUNKS = 2
TURNS = (1, 3, 2)
W = F // CHUNKS
V = W // 2
LEAVE, ARRIVE = 27, 225


def hand_over(*refs):
    half = len(refs) // 2
    for source, target in zip(refs[:half], refs[half:]):
        target[...] = source[...]


def on_device(features, blocks, positions, counts, weight, bias, cotangent):
    smem = pl.BlockSpec(memory_space=pltpu.SMEM)
    anywhere = pl.BlockSpec(memory_space=pl.ANY)
    table = pl.pallas_call(
        link_slots,
        out_shape=jax.ShapeDtypeStruct((TABLE,), jnp.int32),
        in_specs=[smem, smem],
        out_specs=smem,
    )(positions.reshape(SLOTS), counts.reshape(1))

    def chunk(*lead, rows=B, dtype=BF16):
        return pltpu.VMEM((CHUNKS, *lead, rows, W), dtype)

    def part(*lead, rows=B, cols=W, dtype=BF16):
        return pltpu.VMEM((*lead, rows, cols), dtype)

    def pair(*lead, rows=B, dtype=BF16):
        return part(*lead, rows=rows, cols=V, dtype=dtype), part(*lead, rows=rows, dtype=dtype)

    def full(*lead, rows, dtype=F32):
        return pltpu.VMEM((*lead, rows, F), dtype)

    outs = [
        jax.ShapeDtypeStruct((B, F), BF16),
        jax.ShapeDtypeStruct((NK, NX, NH * NY, 8, F), F32),
        jax.ShapeDtypeStruct((1, F), F32),
        jax.ShapeDtypeStruct((B, F), BF16),
    ]
    results = pl.pallas_call(
        layer,
        out_shape=outs,
        in_specs=[anywhere] * 6,
        out_specs=[anywhere] * 4,
        scratch_shapes=[
            pltpu.SMEM((TABLE,), jnp.int32),
            pltpu.VMEM((F, F), BF16),
            pltpu.VMEM((1, F), F32),
            pltpu.VMEM((B, F), BF16),
            pltpu.VMEM((B, F), BF16),
            pltpu.VMEM((1, F), F32),
            pltpu.VMEM((B, F), BF16),
            pltpu.VMEM((SLOTS, B, B), BF16),
            part(TC),
            part(TC),
            chunk(SLOTS + 1, dtype=F32),
            pair(2, NY, rows=HALF),
            pair(2, NY, rows=HALF),
            pair(2, 3, NY),
            pair(2, 3, NY),
            pair(3),
            pair(3),
            pair(dtype=F32),
            part(3, NZ, cols=V),
            part(3, NZ, cols=V),
            part(2, rows=HALF, cols=V),
            part(2, rows=HALF, cols=V),
            part(2, 3, cols=V),
            part(2, 3, cols=V),
            chunk(dtype=F32),
            full(rows=B, dtype=BF16),
            part(TR, cols=V),
            part(TR),
            part(TR, cols=V),
            chunk(8),
            chunk(8),
            chunk(2, 3),
            chunk(2, 3),
            chunk(),
            chunk(),
            full(NK, rows=264),
            full(rows=264),
            full(NX, rows=72),
            full(NX, rows=72),
            full(NH * NY, rows=16),
            full(NH * NY, rows=16),
            full(rows=16, dtype=BF16),
            full(NZ, rows=16, dtype=BF16),
            full(NK, NX, NH * NY, rows=8),
            pltpu.SemaphoreType.DMA((LEAVE,)),
            pltpu.SemaphoreType.DMA((ARRIVE,)),
            pltpu.SemaphoreType.DMA((12,)),
        ],
        compiler_params=pltpu.CompilerParams(
            collective_id=0, has_side_effects=True, vmem_limit_bytes=56 * 2**20
        ),
    )(table, features, blocks.reshape(SLOTS, B, B), weight, bias.reshape(1, F), cotangent)
    vmem = pl.BlockSpec(memory_space=pltpu.VMEM)
    act, gw, gb, gin = pl.pallas_call(hand_over, out_shape=outs, in_specs=[vmem] * 4, out_specs=[vmem] * 4)(*results)
    return act, gw.reshape(F, F), gb.reshape(F), gin


def solution(mesh):
    torus = Mesh(mesh.devices.reshape(NX, NH, NK, NY, NZ), AXES)
    return jax.shard_map(
        on_device,
        mesh=torus,
        in_specs=(
            P(COL_ROW, None),
            P(ROW, COL, None, None, None),
            P(ROW, COL, None),
            P(ROW, COL),
            P(),
            P(),
            P(ROW_COL, None),
        ),
        out_specs=(P(ROW_COL, None), P(), P(), P(COL_ROW, None)),
        check_vma=False,
    )
```

```python
import jax
import jax.numpy as jnp
from jax import lax
from jax.experimental import pallas as pl
from jax.experimental.pallas import tpu as pltpu
from jax.sharding import Mesh
from jax.sharding import PartitionSpec as P

AXES = ("x", "h", "k", "y", "z")
ROW = ("x", "h", "k")
COL = ("y", "z")
ROW_COL = ROW + COL
COL_ROW = COL + ROW
MESH = pl.DeviceIdType.MESH
NX, NH, NK, NY, NZ = 4, 2, 2, 4, 8
TR, TC = NY * NZ, NX * NH * NK
SLOTS = 48
B = 128
HALF = B // 2
F = 512
FC, FP, FL = 0, SLOTS, 2 * SLOTS
BR, BP, BL = FL + TR, FL + TR + SLOTS, FL + TR + 2 * SLOTS
TABLE = BL + TC
BF16, F32 = jnp.bfloat16, jnp.float32


def link_slots(pos, cnt, tab):
    limit = cnt[0]
    for r in range(TR):
        tab[FL + r] = SLOTS
    for c in range(TC):
        tab[BL + c] = SLOTS

    def one(s, carry):
        p = pos[s]
        r, c = lax.div(p, TC), lax.rem(p, TC)
        live = s < limit
        last_r, last_c = tab[FL + r], tab[BL + c]
        tab[FC + s] = c
        tab[BR + s] = r
        tab[FP + s] = last_r
        tab[BP + s] = last_c
        tab[FL + r] = jnp.where(live, s, last_r)
        tab[BL + c] = jnp.where(live, s, last_c)
        return carry

    lax.fori_loop(0, SLOTS, one, 0, unroll=4)


def layer(
    tab_hbm, feat_hbm, blocks_hbm, weight_hbm, bias_hbm, cot_hbm,
    act_hbm, gw_hbm, gb_hbm, gin_hbm,
    tab, weight, bias, cot, act_out, gb_out, gin_out, blocks, fall_0, fall_1, hist, zs1, zr1, zs, zr, ys, yr, oz, y1s, y1r, y2s1, y2r1, y2s, y2r, own_sum, agg, mid_0, mid_1, mid_y, ks, kr, xs, xr, hs, hr,
    g0, gk, gx, gxr, gy, gyr, gz, gzr, gall,
    send, recv, local,
):
    x, h, k, y, z = (lax.axis_index(a) for a in AXES)
    fall, mid = (fall_0, fall_1), (mid_0, mid_1)
    narrow, early, wide = slice(0, V), slice(V, 2 * V), slice(2 * V, F)
    z_cols, z_hist = (narrow, wide), (slice(0, V), slice(0, W))
    own = (lax.axis_index("x") * NH + lax.axis_index("h")) * NK + lax.axis_index("k")
    f_in = [pltpu.make_async_copy(feat_hbm.at[:, pl.ds(c * W, W)], fall[c].at[own], local.at[c]) for c in range(CHUNKS)]
    early_in = [pltpu.make_async_copy(tab_hbm, tab, local.at[2]), pltpu.make_async_copy(blocks_hbm, blocks, local.at[3])]
    late_in = [
        pltpu.make_async_copy(weight_hbm, weight, local.at[4]),
        pltpu.make_async_copy(bias_hbm, bias, local.at[5]),
        pltpu.make_async_copy(cot_hbm, cot, local.at[6]),
    ]
    for c in (*f_in, *early_in, *late_in):
        c.start()
    act_store = pltpu.make_async_copy(act_out, act_hbm, local.at[7])
    gb_store = pltpu.make_async_copy(gb_out, gb_hbm, local.at[8])
    gin_store = pltpu.make_async_copy(gin_out, gin_hbm, local.at[9])
    stores = []

    def store(c):
        c.start()
        stores.append(c)

    def at(name, value):
        return {name: value}

    def xo(d):
        return lax.rem(x + d, NX)

    def zo(d):
        return lax.rem(z + d, NZ)

    def yo(d):
        return lax.rem(y + d, NY)

    hy = h * NY + y

    def y8(d):
        place = lax.rem(hy + d, NH * NY)
        return {"h": lax.div(place, NY), "y": lax.rem(place, NY)}

    other = at("k", 1 - k)
    partner = at("h", 1 - h)
    up, down = at("z", zo(1)), at("z", zo(7))
    ways = ((0, up), (1, down))
    chunks = range(CHUNKS)
    cols = [slice(c * W, (c + 1) * W) for c in chunks]

    barrier = pltpu.get_barrier_semaphore()
    greeted = [other]
    greeted += [at("x", xo(d)) for d in range(1, NX)]
    greeted += [at("z", zo(d)) for d in range(1, NZ)]
    greeted += [y8(d) for d in range(1, NH * NY)]
    for device in greeted:
        pl.semaphore_signal(barrier, inc=1, device_id=device, device_id_type=MESH)

    def place(xx, hh, kk):
        return xx * (NH * NK) + hh * NK + kk

    far = place(x, 1 - h, k)
    for c in chunks:
        hist[c, SLOTS] = jnp.zeros((B, W), F32)
    for c in f_in:
        c.wait()
    pl.semaphore_wait(barrier, len(greeted))

    used, leaving = [0], []

    def ids(count):
        first = used[0]
        used[0] += count
        return first

    def leaves(ref):
        leaving.append(ref)
        return len(leaving) - 1

    def copy(src, dst, device, sent, n):
        return pltpu.make_async_remote_copy(
            src_ref=src, dst_ref=dst, send_sem=send.at[sent], recv_sem=recv.at[n], device_id=device, device_id_type=MESH
        )

    def go(src, dst, device, sent, n=None):
        c = copy(src, dst, device, sent, ids(1) if n is None else n)
        c.start()
        return c

    def received(copies):
        for c in copies:
            c.wait_recv()

    def together(sources, target, devices, ref):
        sent, n = leaves(ref), ids(1)
        for source, device in zip(sources, devices):
            go(source, target, device, sent, n)
        return copy(ref, ref, other, sent, n)

    def features(c):
        sent, cross = leaves(fall[c].at[pl.ds(0, 15)]), ids(1)

        def whole(i, device, n=None):
            return go(fall[c].at[i], fall[c].at[i], device, sent, n)

        to_far = whole(own, partner)
        own_x = [whole(own, at("x", xo(d))) for d in TURNS]
        whole(own, other, cross)
        yield
        to_far.wait_recv()
        far_x = [whole(far, at("x", xo(d))) for d in TURNS]
        whole(far, other, cross)
        yield
        for d, c_x in zip(TURNS, own_x):
            c_x.wait_recv()
            whole(place(xo(NX - d), h, k), other, cross)
        yield
        for d, c_x in zip(TURNS, far_x):
            c_x.wait_recv()
            whole(place(xo(NX - d), 1 - h, k), other, cross)
        yield
        eight = fall[c].at[pl.ds(0, TC // NK)]
        copy(eight, eight, other, sent, cross).wait_recv()
        yield

    step = 8

    def products(c, source, index, before, contract):
        def one(g, carry):
            made = []
            for u in range(step):
                s = g * step + u
                made.append(
                    lax.dot_general(
                        blocks[s],
                        source(tab[index + s]),
                        (((contract,), (0,)), ((), ())),
                        preferred_element_type=F32,
                    )
                )
            for u in range(step):
                s = g * step + u
                hist[c, s] = made[u] + hist[c, tab[before + s]]
            return carry

        lax.fori_loop(0, SLOTS // step, one, 0)

    z_ids = ids(32 * CHUNKS)
    z_sent = [(leaves(zs1[c]), leaves(zs[c])) for c in chunks]

    def z_copy(n, c, w, device, t):
        sem = z_ids + ((c * 4 + n) * 2 + w) * NY + t
        if n == 0:
            return copy(zs1[c].at[w, t], zr1[c].at[w, t], device, z_sent[c][0], sem)
        return copy(zs[c].at[w, n - 1, t], zr[c].at[w, n - 1, t], device, z_sent[c][1], sem)

    def term(c, row, rows=slice(0, B)):
        return hist[c, tab[FL + row], rows, z_hist[c]]

    halves = (slice(0, HALF), slice(HALF, B))

    def scatter_step(n, c):
        def one(t, carry):
            q = yo(1 + t)
            for w, device in ways:
                row = q * NZ + zo(4 - n if w == 0 else 4 + n)
                if n == 0:
                    zs1[c][w, t] = term(c, row, halves[w]).astype(BF16)
                elif n == 1:
                    z_copy(0, c, w, device, t).wait_recv()
                    zs[c][w, 0, t, halves[w]] = (term(c, row, halves[w]) + zr1[c][w, t].astype(F32)).astype(BF16)
                    zs[c][w, 0, t, halves[1 - w]] = term(c, row, halves[1 - w]).astype(BF16)
                else:
                    z_copy(n - 1, c, w, device, t).wait_recv()
                    zs[c][w, n - 1, t] = (term(c, row) + zr[c][w, n - 2, t].astype(F32)).astype(BF16)
                z_copy(n, c, w, device, t).start()
            return carry

        lax.fori_loop(0, NY, one, 0)

    y_copies = []

    def scatter_y(c):
        sent = leaves(ys[c])
        for t in range(NY):
            for w, device in ways:
                z_copy(3, c, w, device, t).wait_recv()
            total = term(c, yo(1 + t) * NZ + z) + zr[c][0, 2, t].astype(F32) + zr[c][1, 2, t].astype(F32)
            if t < NY - 1:
                ys[c][t] = total.astype(BF16)
                y_copies.append(go(ys[c].at[t], yr[c].at[t], at("y", yo(1 + t)), sent))
            else:
                oz[c][...] = total

    order = (4, 3, 5, 2, 6, 1, 7, 0)
    groups = (slice(0, 1), slice(1, 3), slice(3, 5), slice(5, 7), slice(7, 8))
    early_hist = slice(V, 2 * V)
    early_y, early_z = [], {}
    early_sent = [leaves(ref) for ref in (y1s, y2s1, y2s)]

    def early_send():
        for group in groups:
            copies = []
            for d in range(1, NY):
                for p in range(group.start, group.stop):
                    y1s[d - 1, p] = hist[0, tab[FL + yo(d) * NZ + zo(order[p])], :, early_hist].astype(BF16)
                part = pl.ds(group.start, group.stop - group.start)
                copies.append(go(y1s.at[d - 1, part], y1r.at[d - 1, part], at("y", yo(d)), early_sent[0]))
            early_y.append(copies)

    def early_term(p, rows=slice(0, B)):
        total = hist[0, tab[FL + y * NZ + zo(order[p])], rows, early_hist]
        for d in range(NY - 1):
            total += y1r[d, p, rows].astype(F32)
        return total

    def early_step(n):
        received(early_y[n])
        for w, device in ways:
            if n == 0:
                y2s1[w] = early_term(0, halves[w]).astype(BF16)
                early_z[0, w] = go(y2s1.at[w], y2r1.at[w], device, early_sent[1])
                continue
            early_z[n - 1, w].wait_recv()
            p = 2 * n - 1 + w
            if n == 1:
                y2s[w, 0, halves[w]] = (early_term(p, halves[w]) + y2r1[w].astype(F32)).astype(BF16)
                y2s[w, 0, halves[1 - w]] = early_term(p, halves[1 - w]).astype(BF16)
            else:
                y2s[w, n - 1] = (early_term(p) + y2r[w, n - 2].astype(F32)).astype(BF16)
            early_z[n, w] = go(y2s.at[w, n - 1], y2r.at[w, n - 1], device, early_sent[2])

    def early_last():
        received(early_y[4])
        received([early_z[3, 0], early_z[3, 1]])
        agg[:, early] = (early_term(7) + y2r[0, 2].astype(F32) + y2r[1, 2].astype(F32)).astype(BF16)

    first, later = (features(c) for c in chunks)
    next(first)
    next(first)
    next(later)
    next(first)
    next(first)
    next(later)
    next(first)
    for c in early_in:
        c.wait()
    products(0, lambda i: fall[0][i], FC, FP, 1)
    scatter_step(0, 0)
    early_send()
    next(later)
    scatter_step(1, 0)
    next(later)
    scatter_step(2, 0)
    next(later)
    products(1, lambda i: fall[1][i], FC, FP, 1)
    scatter_step(0, 1)
    early_step(0)
    scatter_step(3, 0)
    scatter_step(1, 1)
    early_step(1)
    scatter_y(0)
    scatter_step(2, 1)
    early_step(2)
    scatter_step(3, 1)
    early_step(3)
    scatter_y(1)
    early_last()
    received(y_copies)
    for c in chunks:
        agg[:, z_cols[c]] = (
            oz[c][...] + yr[c][0].astype(F32) + yr[c][1].astype(F32) + yr[c][2].astype(F32)
        ).astype(BF16)

    for c in late_in:
        c.wait()
    pre = jnp.dot(agg[...], weight[...], preferred_element_type=F32) + bias[...]
    sigma = jax.nn.sigmoid(pre)
    act_out[...] = (pre * sigma).astype(BF16)
    store(act_store)
    grad_pre = (cot[...].astype(F32) * sigma * (1.0 + pre * (1.0 - sigma))).astype(BF16)
    mine = y * NZ + z
    m_ids = ids(32 * CHUNKS)
    m_sent = [leaves(mid[c].at[pl.ds(0, 31)]) for c in chunks]

    def m_copy(n, c, w, device, t):
        row = yo(NY - t) * NZ + zo(NZ - n if w == 0 else n)
        sem = m_ids + ((c * 4 + n) * 2 + w) * NY + t
        ref = mid[c].at[row]
        if n == 3:
            ref = mid[c].at[row, pl.ds(w * HALF, HALF)]
        return copy(ref, ref, device, m_sent[c], sem)

    def grad_mid(part):
        return lax.dot_general(
            grad_pre, weight[part, :], (((1,), (1,)), ((), ())), preferred_element_type=F32
        ).astype(BF16)

    m_y = {}
    e_ids, e_y = ids(8), ids(1)
    e_sent = leaves(mid_y.at[pl.ds(0, 31)])

    def e_copy(n, w, device):
        row = y * NZ + zo(NZ - n if w == 0 else n)
        ref = mid_y.at[row]
        if n == 3:
            ref = mid_y.at[row, pl.ds(w * HALF, HALF)]
        return copy(ref, ref, device, e_sent, e_ids + n * 2 + w)

    def e_spread(row):
        for t in range(1, NY):
            go(mid_y.at[row], mid_y.at[row], at("y", yo(t)), e_sent, e_y)

    def early_gather(n):
        for w, device in ways:
            if n > 0:
                e_copy(n - 1, w, device).wait_recv()
            if n < 4:
                e_copy(n, w, device).start()
        if n == 0:
            e_spread(mine)
        elif n < 4:
            e_spread(y * NZ + zo(NZ - n))
            e_spread(y * NZ + zo(n))
        else:
            e_spread(y * NZ + zo(4))

    for c in (1, 0):
        mid[c][mine] = grad_mid(z_cols[c])
        if c == 1:
            for w, device in ways:
                m_copy(0, c, w, device, 0).start()
        m_y[c] = [go(mid[c].at[mine], mid[c].at[mine], at("y", yo(t)), m_sent[c]) for t in range(1, NY)]
        if c == 1:
            mid_y[mine] = grad_mid(early)
            early_gather(0)

    def gather_first(c):
        if c == 0:
            for w, device in ways:
                m_copy(0, c, w, device, 0).start()
        for t in range(1, NY):
            m_y[c][t - 1].wait_recv()
            for w, device in ways:
                m_copy(0, c, w, device, t).start()

    def gather_step(n, c):
        def one(t, carry):
            for w, device in ways:
                m_copy(n - 1, c, w, device, t).wait_recv()
                m_copy(n, c, w, device, t).start()
            return carry

        lax.fori_loop(0, NY, one, 0)

    def gather_last(c):
        def one(t, carry):
            for w, device in ways:
                m_copy(3, c, w, device, t).wait_recv()
            return carry

        lax.fori_loop(0, NY, one, 0)

    def gradients():
        gb = jnp.sum(grad_pre.astype(F32), axis=0, keepdims=True)
        bias_rows = jnp.broadcast_to(gb, (8, F))
        for kk in range(NK):
            g0[kk, 0:256] = lax.dot_general(
                agg[:, kk * 256 : (kk + 1) * 256], grad_pre, (((0,), (0,)), ((), ())), preferred_element_type=F32
            )
            g0[kk, 256:264] = bias_rows
        k_copy = go(g0.at[1 - k], gk, other, leaves(gk))
        yield
        k_copy.wait_recv()
        for i in range(NX):
            gx[i, 0:64] = g0[k, i * 64 : (i + 1) * 64] + gk[i * 64 : (i + 1) * 64]
            gx[i, 64:72] = g0[k, 256:264] + gk[256:264]
        gxr[x] = gx[x]
        x_devices = [at("x", xo(d)) for d in range(1, NX)]
        y_devices = [y8(d) for d in range(1, NH * NY)]
        copies = together([gx.at[xo(d)] for d in range(1, NX)], gxr.at[x], x_devices, gxr.at[pl.ds(0, 3)])
        yield
        copies.wait_recv()
        bias_sum = gxr[0, 64:72] + gxr[1, 64:72] + gxr[2, 64:72] + gxr[3, 64:72]
        for i in range(NH * NY):
            rows = slice(i * 8, (i + 1) * 8)
            gy[i, 0:8] = gxr[0, rows] + gxr[1, rows] + gxr[2, rows] + gxr[3, rows]
            gy[i, 8:16] = bias_sum
        gyr[hy] = gy[hy]
        sources = [gy.at[lax.rem(hy + d, NH * NY)] for d in range(1, NH * NY)]
        copies = together(sources, gyr.at[hy], y_devices, gyr.at[pl.ds(0, 7)])
        yield
        copies.wait_recv()
        total = gyr[0]
        for i in range(1, NH * NY):
            total += gyr[i]
        gz[...] = total.astype(BF16)
        gzr[z] = gz[...]
        copies = together([gz] * 7, gzr.at[z], [at("z", zo(d)) for d in range(1, NZ)], gzr.at[pl.ds(0, 7)])
        yield
        copies.wait_recv()
        total = gzr[0].astype(F32)
        for i in range(1, NZ):
            total += gzr[i].astype(F32)
        gb_out[...] = total[8:9]
        store(gb_store)
        gall[k, x, hy] = total[0:8]
        piece = gall.at[k, x, hy]
        copies = together([piece] * 7, piece, y_devices, gall.at[0, 0, pl.ds(0, 7)])
        yield
        copies.wait_recv()
        piece = gall.at[k, x]
        copies = together([piece] * 3, piece, x_devices, gall.at[0, pl.ds(0, 3)])
        yield
        copies.wait_recv()
        k_copy = go(gall.at[k], gall.at[k], other, leaves(gall.at[0]))
        store(pltpu.make_async_copy(gall.at[k], gw_hbm.at[k], local.at[10]))
        yield
        k_copy.wait_recv()
        store(pltpu.make_async_copy(gall.at[1 - k], gw_hbm.at[1 - k], local.at[11]))
        yield

    def hp(dh):
        return 1 - h if dh else h

    turns = [(dh, dx) for dh in (1, 0) for dx in (*TURNS, 0)]

    def back(c):
        sent_k, sent_x = leaves(ks.at[c]), leaves(xs.at[c])
        k_copies = []
        for j, (dh, dx) in enumerate(turns):
            ks[c, j] = hist[c, tab[BL + place(xo(dx), hp(dh), 1 - k)]].astype(BF16)
            k_copies.append(go(ks.at[c, j], kr.at[c, j], other, sent_k))
        yield

        def back_term(j):
            dh, dx = turns[j]
            return hist[c, tab[BL + place(xo(dx), hp(dh), k)]] + kr[c, j].astype(F32)

        def x_sends(dh):
            copies = []
            for j, (dj, dx) in enumerate(turns):
                if dj == dh:
                    k_copies[j].wait_recv()
                    if dx:
                        xs[c, dh, dx - 1] = back_term(j).astype(BF16)
                        copies.append(go(xs.at[c, dh, dx - 1], xr.at[c, dh, dx - 1], at("x", xo(dx)), sent_x))
            return copies

        def x_sum(dh, copies):
            received(copies)
            total = back_term(turns.index((dh, 0)))
            for i in range(NX - 1):
                total += xr[c, dh, i].astype(F32)
            return total

        copies = x_sends(1)
        yield
        hs[c] = x_sum(1, copies).astype(BF16)
        h_copy = go(hs.at[c], hr.at[c], partner, leaves(hs.at[c]))
        copies = x_sends(0)
        yield
        own_sum[c] = x_sum(0, copies)
        yield
        h_copy.wait_recv()
        gin_out[:, cols[c]] = (own_sum[c] + hr[c].astype(F32)).astype(BF16)
        yield

    grads = gradients()
    backs = [back(c) for c in chunks]
    gather_first(1)
    next(grads)
    early_gather(1)
    gather_step(1, 1)
    next(grads)
    early_gather(2)
    gather_step(2, 1)
    early_gather(3)
    gather_step(3, 1)
    next(grads)
    gather_first(0)
    early_gather(4)
    gather_last(1)
    gather_step(1, 0)
    products(1, lambda i: mid[1][i], BR, BP, 0)
    next(backs[1])
    gather_step(2, 0)
    next(backs[1])
    next(grads)
    gather_step(3, 0)
    next(backs[1])
    next(backs[1])
    gather_last(0)
    most = mid_y.at[pl.ds(0, NZ * (NY - 1))]
    copy(most, most, up, e_sent, e_y).wait_recv()
    next(grads)
    products(0, lambda i: jnp.concatenate([mid[0][i], mid_y[i]], axis=1), BR, BP, 0)
    next(backs[0])
    next(backs[1])
    next(backs[0])
    next(grads)
    next(backs[0])
    next(backs[0])
    next(grads)
    next(backs[0])
    store(gin_store)
    next(grads)
    for c in stores:
        c.wait()

    for n, ref in enumerate(leaving):
        copy(ref, ref, other, n, 0).wait_send()
    assert used[0] == ARRIVE and len(leaving) == LEAVE


CHUNKS = 2
TURNS = (1, 3, 2)
W = F // CHUNKS
V = W // 2
LEAVE, ARRIVE = 27, 225


def hand_over(*refs):
    half = len(refs) // 2
    for source, target in zip(refs[:half], refs[half:]):
        target[...] = source[...]


def on_device(features, blocks, positions, counts, weight, bias, cotangent):
    smem = pl.BlockSpec(memory_space=pltpu.SMEM)
    anywhere = pl.BlockSpec(memory_space=pl.ANY)
    table = pl.pallas_call(
        link_slots,
        out_shape=jax.ShapeDtypeStruct((TABLE,), jnp.int32),
        in_specs=[smem, smem],
        out_specs=smem,
    )(positions.reshape(SLOTS), counts.reshape(1))

    def chunk(*lead, rows=B, dtype=BF16):
        return pltpu.VMEM((CHUNKS, *lead, rows, W), dtype)

    def part(*lead, rows=B, cols=W, dtype=BF16):
        return pltpu.VMEM((*lead, rows, cols), dtype)

    def pair(*lead, rows=B, dtype=BF16):
        return part(*lead, rows=rows, cols=V, dtype=dtype), part(*lead, rows=rows, dtype=dtype)

    def full(*lead, rows, dtype=F32):
        return pltpu.VMEM((*lead, rows, F), dtype)

    outs = [
        jax.ShapeDtypeStruct((B, F), BF16),
        jax.ShapeDtypeStruct((NK, NX, NH * NY, 8, F), F32),
        jax.ShapeDtypeStruct((1, F), F32),
        jax.ShapeDtypeStruct((B, F), BF16),
    ]
    results = pl.pallas_call(
        layer,
        out_shape=outs,
        in_specs=[anywhere] * 6,
        out_specs=[anywhere] * 4,
        scratch_shapes=[
            pltpu.SMEM((TABLE,), jnp.int32),
            pltpu.VMEM((F, F), BF16),
            pltpu.VMEM((1, F), F32),
            pltpu.VMEM((B, F), BF16),
            pltpu.VMEM((B, F), BF16),
            pltpu.VMEM((1, F), F32),
            pltpu.VMEM((B, F), BF16),
            pltpu.VMEM((SLOTS, B, B), BF16),
            part(TC),
            part(TC),
            chunk(SLOTS + 1, dtype=F32),
            pair(2, NY, rows=HALF),
            pair(2, NY, rows=HALF),
            pair(2, 3, NY),
            pair(2, 3, NY),
            pair(3),
            pair(3),
            pair(dtype=F32),
            part(3, NZ, cols=V),
            part(3, NZ, cols=V),
            part(2, rows=HALF, cols=V),
            part(2, rows=HALF, cols=V),
            part(2, 3, cols=V),
            part(2, 3, cols=V),
            chunk(dtype=F32),
            full(rows=B, dtype=BF16),
            part(TR, cols=V),
            part(TR),
            part(TR, cols=V),
            chunk(8),
            chunk(8),
            chunk(2, 3),
            chunk(2, 3),
            chunk(),
            chunk(),
            full(NK, rows=264),
            full(rows=264),
            full(NX, rows=72),
            full(NX, rows=72),
            full(NH * NY, rows=16),
            full(NH * NY, rows=16),
            full(rows=16, dtype=BF16),
            full(NZ, rows=16, dtype=BF16),
            full(NK, NX, NH * NY, rows=8),
            pltpu.SemaphoreType.DMA((LEAVE,)),
            pltpu.SemaphoreType.DMA((ARRIVE,)),
            pltpu.SemaphoreType.DMA((12,)),
        ],
        compiler_params=pltpu.CompilerParams(
            collective_id=0, has_side_effects=True, vmem_limit_bytes=56 * 2**20
        ),
    )(table, features, blocks.reshape(SLOTS, B, B), weight, bias.reshape(1, F), cotangent)
    vmem = pl.BlockSpec(memory_space=pltpu.VMEM)
    act, gw, gb, gin = pl.pallas_call(hand_over, out_shape=outs, in_specs=[vmem] * 4, out_specs=[vmem] * 4)(*results)
    return act, gw.reshape(F, F), gb.reshape(F), gin


def solution(mesh):
    torus = Mesh(mesh.devices.reshape(NX, NH, NK, NY, NZ), AXES)
    return jax.shard_map(
        on_device,
        mesh=torus,
        in_specs=(
            P(COL_ROW, None),
            P(ROW, COL, None, None, None),
            P(ROW, COL, None),
            P(ROW, COL),
            P(),
            P(),
            P(ROW_COL, None),
        ),
        out_specs=(P(ROW_COL, None), P(), P(), P(COL_ROW, None)),
        check_vma=False,
    )
```
